128 devices in a mesh: fsdp: 8 (over z, core), ctx: 8 (over x, y_lo), tp: 2 (over y_hi).
Axes of the slice: x: 4, y: 4 (y_hi: 2, y_lo: 2; y = y_hi * 2 + y_lo), z: 4, core: 2. Of those that a mesh axis runs over, the one named last changes fastest.
Arguments:
- inputs: bfloat16 [8192, 2048], P(('fsdp', 'ctx')), may hold values from -6 to 6
- lengths: int32 [8], replicated, may hold values from 1 to 1024, 5120 in all
- routes: int32 [8192, 4], P(('fsdp', 'ctx')), may hold values from 0 to 7, all different within a row; in each aligned block of 128 rows (0 to 127, 128 to 255, ...) at most 80 rows name the same one
- norm_gains: bfloat16 [2, 2048], P(None, 'fsdp'), may hold values from 0.5 to 1.5
- w_qkv: bfloat16 [2048, 3, 2048], P('fsdp', None, 'tp'), may hold values from -0.125 to 0.125
- b_qkv: bfloat16 [3, 16, 128], P(None, 'tp', 'fsdp'), may hold values from -1.1953125 to 1.1953125
- w_o: bfloat16 [2048, 2048], P('fsdp', 'tp'), may hold values from -0.5 to 0.5
- w_router: bfloat16 [2048, 8], P('fsdp'), may hold values from -0.0625 to 0.0625
- w_sgate: bfloat16 [2048], P('fsdp'), may hold values from -0.125 to 0.125
- w_sgu: bfloat16 [2048, 2, 5632], P('fsdp', None, 'tp'), may hold values from -0.125 to 0.125
- w_sdown: bfloat16 [2048, 5632], P('fsdp', 'tp'), may hold values from -0.15625 to 0.15625
- w_egu: bfloat16 [2048, 8, 2, 1408], P('fsdp', None, None, 'tp'), may hold values from -0.125 to 0.125
- w_edown: bfloat16 [2048, 8, 1408], P('fsdp', None, 'tp'), may hold values from -0.4375 to 0.4375
- grad_out: bfloat16 [8192, 2048], P(('fsdp', 'ctx')), may hold values from -6 to 6
Outputs:
- output: bfloat16 [8192, 2048], P(('fsdp', 'ctx'))
- grad_inputs: bfloat16 [8192, 2048], P(('fsdp', 'ctx'))
- grad_norm_gains: float32 [2, 2048], P(None, 'fsdp')
- grad_w_qkv: float32 [2048, 3, 2048], P('fsdp', None, 'tp')
- grad_b_qkv: float32 [3, 16, 128], P(None, 'tp', 'fsdp')
- grad_w_o: float32 [2048, 2048], P('fsdp', 'tp')
- grad_w_router: float32 [2048, 8], P('fsdp')
- grad_w_sgate: float32 [2048], P('fsdp')
- grad_w_sgu: float32 [2048, 2, 5632], P('fsdp', None, 'tp')
- grad_w_sdown: float32 [2048, 5632], P('fsdp', 'tp')
- grad_w_egu: float32 [2048, 8, 2, 1408], P('fsdp', None, None, 'tp')
- grad_w_edown: float32 [2048, 8, 1408], P('fsdp', None, 'tp')
The draws below stay inside these ranges and needn't reach their ends.
Inputs may be any that keep to these rules, and one draw needn't show every extreme that they name: `lengths`: each sequence's count of valid tokens; the longest has all 1024 slots. `routes`: each row names 4 different experts; within the rows of one device no expert is named by more than 80 rows, a bound that some block reaches.
All inputs are finite; a program needn't handle non-finite values.
Results may differ from the reference program's by a relative error of at most 0.029.
Values may be sent and summed in bfloat16 or wider, within the bound.
No kernel may reach another device: no remote copies, remote signals or barrier semaphores. Data moves between devices by JAX's collectives and lax.ppermute only.
A program may use at most 384 MiB of HBM per device.

```python
import math
import jax
import jax.numpy as jnp
import numpy as np
from jax import lax

D = 2048
H = 16
HD = 128
F = 1408
FS = 5632
E = 8
TOPK = 4
SEQ = 1024
TOK_DEV = 128
TOKENS = 8192
CAP = 80
N_FSDP = 8


def block_scale(stream_key, shape, shards, low, top_value):
    factor_of, own = 1.0, jax.random.fold_in(stream_key, 6)
    for position, shards_of in shards:
        draws = jnp.exp(jax.random.uniform(jax.random.fold_in(own, position), (shards_of,), jnp.float32, low / len(shards), top_value / len(shards)))
        factor_of = factor_of * jnp.repeat(draws, shape[position] // shards_of).reshape([-1 if axis == position else 1 for axis in range(len(shape))])
    return factor_of


def profile(amount, total, reach, skew):
    weights = [(1 << 20) // math.isqrt(rank ** skew) + 1 for rank in range(2, amount + 1)]
    spare, holding = total - reach - (amount - 1), [1] * (amount - 1)
    while spare > 0:
        candidates = [i for i in range(amount - 1) if holding[i] < reach]
        mass, remaining = sum([weights[i] for i in candidates]), spare
        for i in candidates:
            more = min(reach - holding[i], max(1, remaining * weights[i] // mass), spare)
            holding[i] = holding[i] + more
            spare = spare - more
    return np.array([reach] + holding)


def ragged(rng, count, total, reach, slope):
    if count == 2:
        one = jax.random.randint(rng, (), max(1, total - reach), min(reach, total - 1) + 1)
        return jnp.stack([one, total - one])
    tallies = jnp.asarray(profile(count, total, reach, slope), jnp.int32)
    couples = (count - 1) // 2
    giver, sink = tallies[1:1 + 2 * couples:2], tallies[2:2 + 2 * couples:2]
    room = jnp.minimum(giver - 1, reach - sink)
    passed = jax.random.randint(jax.random.fold_in(rng, 1), (couples,), 0, 1 << 20) % (room + 1)
    tallies = tallies.at[1:1 + 2 * couples:2].set(giver - passed).at[2:2 + 2 * couples:2].set(sink + passed)
    return tallies[jax.random.permutation(jax.random.fold_in(rng, 2), count)]


def routed_block(stream_key, own, number, rows, amount, top, limit, slope):
    order = jax.random.permutation(stream_key, amount)
    crowded, usual = portions_of(amount, rows * top, limit, slope, True), portions_of(amount, rows * top, limit, slope, False)
    places = jnp.arange(amount)

    def named(sizes, rotation):
        used = int((sizes > 0).sum())
        fixed = max(1, used // 4)
        moved = fixed + (places - fixed + rotation * (used - fixed)) % max(1, amount - fixed)
        return jnp.zeros((amount,), jnp.int32).at[order[jnp.where(places < fixed, places, moved)]].set(jnp.asarray(sizes, jnp.int32))

    sizes = jnp.where(number % 4 == 0, named(crowded, number // 4), named(usual, number - number // 4 - 1))
    mixed = jax.random.permutation(jax.random.fold_in(own, 3), amount)
    source_of, taker = mixed[0:amount // 2 * 2:2], mixed[1:amount // 2 * 2:2]
    slack = jnp.minimum(sizes[source_of] - 1, limit - sizes[taker]) // 2
    slack = jnp.where((source_of == order[0]) | (taker == order[0]) | (sizes[taker] == 0), 0, jnp.maximum(slack, 0))
    moved = jax.random.randint(jax.random.fold_in(own, 4), (amount // 2,), 0, 1 << 20) % (slack + 1)
    sizes = sizes.at[source_of].add(-moved).at[taker].add(moved)
    items = jnp.searchsorted(jnp.cumsum(sizes), jnp.arange(rows * top), side="right").astype(jnp.int32)
    table = items.reshape(top, rows).T
    table = table[jax.random.permutation(jax.random.fold_in(own, 1), rows)]
    rotation = jax.random.randint(jax.random.fold_in(own, 2), (rows, 1), 0, top)
    return jnp.take_along_axis(table, (jnp.arange(top)[None, :] + rotation) % top, axis=1)


def portions_of(amount, total, bound, lean, full):
    weights = [(1 << 20) // math.isqrt(grade ** lean) + 1 for grade in range(1, amount + 1)]
    largest = bound if full else min(bound, max(-(-total // amount), total * weights[0] // sum(weights)))
    least = 1 if total - largest >= amount - 1 else 0
    given, rest = [largest] + [least] * (amount - 1), total - largest - least * (amount - 1)
    while rest > 0:
        candidates = [i for i in range(1, amount) if given[i] < largest] or [i for i in range(1, amount) if given[i] < bound]
        pool, left = sum([weights[i] for i in candidates]), rest
        for i in candidates:
            addition = min(bound - given[i], max(1, left * weights[i] // pool), rest)
            given[i] = given[i] + addition
            rest = rest - addition
    return np.array(given)


def noise(own_key, dims, width, bound, split=(), kind=jnp.bfloat16):
    drawn = width * jax.random.normal(own_key, dims, jnp.float32)
    if split:
        drawn = drawn * block_scale(own_key, dims, split, -0.22, 0.18)
    return jnp.clip(drawn, -bound, bound).astype(kind)


def setup_inputs(seed: int = 0) -> dict:
    keys = jax.random.split(jax.random.key(seed), 15)
    inputs = noise(keys[0], (TOKENS, D), 1.0, 6.0, ((0, 64),))
    lengths = ragged(keys[1], N_FSDP, N_FSDP * SEQ * 5 // 8, SEQ, 1).astype(jnp.int32)
    routes_keys = jax.random.split(jax.random.fold_in(keys[2], 1), TOKENS // TOK_DEV)
    routes_turns = jax.random.permutation(jax.random.fold_in(keys[2], 3), TOKENS // TOK_DEV)
    routes = jax.vmap(lambda own, number: routed_block(jax.random.fold_in(keys[2], 2), own, number, TOK_DEV, E, TOPK, CAP, 1))(routes_keys, routes_turns).reshape((TOKENS, TOPK))
    norm_gains = jnp.clip(1.0 + 0.1 * jax.random.normal(keys[3], (2, D), jnp.float32), 0.5, 1.5).astype(jnp.bfloat16)
    w_qkv = noise(keys[4], (D, 3, D), D ** -0.5, 0.125, ((0, 8), (2, 2)))
    b_qkv = noise(keys[5], (3, H, HD), 0.2, 1.1953125, ((1, 2), (2, 8)))
    w_o = noise(keys[6], (D, D), (D // 16) ** -0.5, 0.5, ((0, 8), (1, 2)))
    w_router = noise(keys[7], (D, E), (4 * D) ** -0.5, 0.0625, ((0, 8),))
    w_sgate = noise(keys[8], (D,), D ** -0.5, 0.125, ((0, 8),))
    w_sgu = noise(keys[9], (D, 2, FS), D ** -0.5, 0.125, ((0, 8), (2, 2)))
    w_sdown = noise(keys[10], (D, FS), (FS // 4) ** -0.5, 0.15625, ((0, 8), (1, 2)))
    w_egu = noise(keys[11], (D, E, 2, F), D ** -0.5, 0.125, ((0, 8), (3, 2)))
    w_edown = noise(keys[12], (D, E, F), (F // 8) ** -0.5, 0.4375, ((0, 8), (2, 2)))
    grad_out = noise(keys[13], (TOKENS, D), 1.0, 6.0, ((0, 64),))
    return dict(inputs=inputs, lengths=lengths, routes=routes, norm_gains=norm_gains, w_qkv=w_qkv, b_qkv=b_qkv, w_o=w_o, w_router=w_router, w_sgate=w_sgate, w_sgu=w_sgu, w_sdown=w_sdown, w_egu=w_egu, w_edown=w_edown, grad_out=grad_out)


EPSILON = 1e-06
ROPE_BASE = 1000000.0
MASKED_SCORE = -1e+30

@jax.custom_vjp
def low(v):
    return lax.optimization_barrier(v.astype(jnp.bfloat16)).astype(jnp.float32)

@jax.custom_vjp
def low_back(v):
    return v

def low_keep(v):
    return (low(v), None)

def low_pass(kept, grad):
    return (grad,)

def back_keep(v):
    return (v, None)

def back_low(kept, grad):
    return (low(grad),)
low.defvjp(low_keep, low_pass)
low_back.defvjp(back_keep, back_low)

def rotary_tables(row_count, offset, head_size):
    middle = head_size // 2
    inverse = ROPE_BASE ** (-(jnp.arange(middle, dtype=jnp.float32) * 2.0) / head_size)
    places = (offset + jnp.arange(row_count, dtype=jnp.int32)).astype(jnp.float32)
    angles = places[:, None] * inverse[None, :]
    angles = jnp.concatenate([angles, angles], axis=-1)
    return (jnp.cos(angles), jnp.sin(angles))

def rotate(values, cosine_table, sine_table):
    middle = values.shape[-1] // 2
    turned = jnp.concatenate([-values[..., middle:], values[..., :middle]], axis=-1)
    return values * cosine_table[:, None, :] + turned * sine_table[:, None, :]

def inverse_rms(values):
    return lax.rsqrt(lax.optimization_barrier(jnp.mean(values * values, axis=-1, keepdims=True)) + EPSILON)

def swiglu(pre_act):
    return jax.nn.silu(pre_act[:, 0]) * pre_act[:, 1]

def forward(params, hidden_in, valid_rows, chosen):
    norm_gains, w_qkv, b_qkv, w_o, w_router, w_sgate, w_sgu, w_sdown, w_egu, w_edown = params
    highest = lax.Precision.HIGHEST
    normed_first = low(hidden_in * inverse_rms(hidden_in) * norm_gains[0])
    projected = jnp.einsum('td,dcf->tcf', normed_first, w_qkv, precision=highest) + b_qkv.reshape(3, D)
    projected = low_back(projected).reshape(SEQ, 3, H, HD)
    cosine_table, sine_table = rotary_tables(SEQ, 0, HD)
    queries = low(rotate(projected[:, 0], cosine_table, sine_table))
    key_rows = low(rotate(projected[:, 1], cosine_table, sine_table))
    values = low(projected[:, 2])
    scores = low_back(jnp.einsum('qhe,khe->hqk', queries, key_rows, precision=highest) * HD ** (-0.5))
    places = jnp.arange(SEQ, dtype=jnp.int32)
    causal = places[None, :] <= places[:, None]
    scores = jnp.where(causal[None], scores, MASKED_SCORE)
    att_probs = low(jax.nn.softmax(scores, axis=-1))
    attended = jnp.einsum('hqk,khe->qhe', att_probs, values, precision=highest).reshape(SEQ, D)
    attended = low_back(low(attended))
    branch = low_back(jnp.dot(attended, w_o.T, precision=highest))
    middle_state = hidden_in + branch
    normed_second = low(middle_state * inverse_rms(middle_state) * norm_gains[1])
    logits = low_back(jnp.dot(normed_second, w_router, precision=highest))
    combine = chosen * jax.nn.softmax(logits, axis=-1)
    shared_gate = jax.nn.sigmoid(low_back(jnp.dot(normed_second, w_sgate, precision=highest)))
    shared_pre = low_back(jnp.einsum('td,dcf->tcf', normed_second, w_sgu, precision=highest))
    shared_hidden = low(swiglu(shared_pre))
    shared_out = low_back(jnp.dot(shared_hidden, w_sdown.T, precision=highest))
    mixed_sum = shared_gate[:, None] * shared_out
    for expert in range(E):
        expert_pre = low_back(jnp.einsum('td,dcf->tcf', normed_second, w_egu[:, expert], precision=highest))
        expert_hidden = low(swiglu(expert_pre))
        expert_out = low_back(jnp.dot(expert_hidden, w_edown[:, expert].T, precision=highest))
        mixed_sum = mixed_sum + combine[:, expert:expert + 1] * expert_out
    return valid_rows[:, None] * (middle_state + mixed_sum)

def reference(inputs, lengths, routes, norm_gains, w_qkv, b_qkv, w_o, w_router, w_sgate, w_sgu, w_sdown, w_egu, w_edown, grad_out):
    params = tuple((weight.astype(jnp.float32) for weight in (norm_gains, w_qkv, b_qkv, w_o, w_router, w_sgate, w_sgu, w_sdown, w_egu, w_edown)))
    hidden_all = inputs.astype(jnp.float32).reshape(N_FSDP, SEQ, D)
    grads_all = grad_out.astype(jnp.float32).reshape(N_FSDP, SEQ, D)
    routes_all = routes.reshape(N_FSDP, SEQ, TOPK)
    experts_range = jnp.arange(E, dtype=jnp.int32)

    def per_sequence(totals, sequence_item):
        hidden_in, grad_seq, route_seq, length = sequence_item
        valid_rows = (jnp.arange(SEQ, dtype=jnp.int32) < length).astype(jnp.float32)
        chosen = jnp.any(route_seq[:, :, None] == experts_range[None, None, :], axis=1).astype(jnp.float32) * valid_rows[:, None]
        result, pullback = jax.vjp(lambda weights, state: forward(weights, state, valid_rows, chosen), params, hidden_in)
        grad_weights, grad_state = pullback(grad_seq)
        totals = jax.tree.map(lambda running, addend: running + addend, totals, grad_weights)
        return (totals, (result, grad_state))
    zero_grads = jax.tree.map(jnp.zeros_like, params)
    totals, (results, grad_states) = lax.scan(per_sequence, zero_grads, (hidden_all, grads_all, routes_all, lengths))
    return (results.reshape(TOKENS, D).astype(jnp.bfloat16), grad_states.reshape(TOKENS, D).astype(jnp.bfloat16), totals[0], totals[1], totals[2], totals[3], totals[4], totals[5], totals[6], totals[7], totals[8], totals[9])
```

```python
import jax
import jax.numpy as jnp
from jax import lax
from jax.experimental import pallas as pl
from jax.experimental.pallas import tpu as pltpu
from jax.sharding import PartitionSpec as P

EPSILON = 1e-06
ROPE_BASE = 1000000.0
MASKED_SCORE = -1e30
LOW = jnp.bfloat16
WIDE = jnp.float32
VMEM_BYTES = 56 * 1024 * 1024


def low(values):
    return values.astype(LOW)


def wide(values):
    return values.astype(WIDE)


def rotary_tables(row_count, head_size):
    middle = head_size // 2
    inverse = ROPE_BASE ** (-(jnp.arange(middle, dtype=WIDE) * 2.0) / head_size)
    places = jnp.arange(row_count, dtype=jnp.int32).astype(WIDE)
    angles = places[:, None] * inverse[None, :]
    cosine, sine = jnp.cos(angles), jnp.sin(angles)
    return (
        jnp.concatenate([cosine, cosine], axis=-1),
        jnp.concatenate([-sine, sine], axis=-1),
    )


def inverse_rms(values):
    return lax.rsqrt(jnp.mean(values * values, axis=-1, keepdims=True) + EPSILON)


def ring(step):
    return [(i, (i + step) % 8) for i in range(8)]


PAIR = [(i, i ^ 1) for i in range(8)]


def up(values):
    return lax.ppermute(values, "ctx", ring(2))


def down(values):
    return lax.ppermute(values, "ctx", ring(-2))


def swap(values):
    return lax.ppermute(values, "ctx", PAIR)


def relative_places():
    here = lax.axis_index("ctx")
    return [(here + step) % 8 for step in (0, 6, 2, 4)] + [
        ((here ^ 1) + step) % 8 for step in (0, 6, 2, 4)
    ]


def gather_relative(block):
    half = block.shape[0] // 2
    left, right, pair = up(block), down(block), swap(block)
    first, second = up(left[:half]), down(right[half:])
    pair_left, pair_right = up(pair), down(pair)
    opposite = jnp.concatenate([first, second], axis=0)
    pair_opposite = swap(opposite)
    return [block, left, right, opposite, pair, pair_left, pair_right, pair_opposite]


def in_order(blocks):
    placed = jnp.zeros((8,) + blocks[0].shape, blocks[0].dtype)
    for block, place in zip(blocks, relative_places()):
        placed = lax.dynamic_update_slice(placed, block[None], (place,) + (0,) * block.ndim)
    return placed


def scatter_relative(blocks):
    own, left, right, opposite, pair, pair_left, pair_right, pair_opposite = blocks
    half = own.shape[0] // 2
    from_pair = swap(low(pair_opposite))
    pair_up, pair_down = up(low(pair_right)), down(low(pair_left))
    opposite = wide(opposite) + wide(from_pair)
    first, second = up(low(opposite[:half])), down(low(opposite[half:]))
    crossing = swap(low(wide(pair) + wide(pair_up) + wide(pair_down)))
    right = jnp.concatenate([wide(right[:half]) + wide(first), wide(right[half:])], axis=0)
    left = jnp.concatenate([wide(left[:half]), wide(left[half:]) + wide(second)], axis=0)
    last_up, last_down = up(low(right)), down(low(left))
    return wide(own) + wide(crossing) + wide(last_up) + wide(last_down)


def add_halves(values):
    mine = low(values)
    return wide(mine) + wide(lax.ppermute(mine, "tp", [(0, 1), (1, 0)]))


QUERY_ROWS = 256


def turn(values, cosine, sine):
    return values * cosine + pltpu.roll(values, values.shape[-1] // 2, 1) * sine


def dot_rows(left, right):
    return lax.dot_general(left, right, (((1,), (1,)), ((), ())), preferred_element_type=WIDE)


def dot_columns(left, right):
    return lax.dot_general(left, right, (((0,), (0,)), ((), ())), preferred_element_type=WIDE)


def probabilities(queries, keys, start, scale):
    scores = dot_rows(queries, keys) * scale
    rows = start + lax.broadcasted_iota(jnp.int32, scores.shape, 0)
    columns = lax.broadcasted_iota(jnp.int32, scores.shape, 1)
    scores = jnp.where(columns <= rows, scores, MASKED_SCORE)
    expons = jnp.exp(scores - jnp.max(scores, axis=-1, keepdims=True))
    return expons / jnp.sum(expons, axis=-1, keepdims=True)


def attend_kernel(proj_ref, cos_ref, sin_ref, q_ref, k_ref, v_ref, out_ref):
    size = cos_ref.shape[1]
    scale = size ** (-0.5)
    cosine, sine = cos_ref[...], sin_ref[...]
    q_ref[...] = low(turn(proj_ref[:, :size], cosine, sine))
    k_ref[...] = low(turn(proj_ref[:, size : 2 * size], cosine, sine))
    v_ref[...] = low(proj_ref[:, 2 * size :])
    for start in range(0, q_ref.shape[0], QUERY_ROWS):
        end = start + QUERY_ROWS
        probs = low(probabilities(q_ref[start:end], k_ref[:end], start, scale))
        out_ref[start:end] = low(jnp.dot(probs, v_ref[:end], preferred_element_type=WIDE))


def attend_back_kernel(
    q_ref, k_ref, v_ref, grad_ref, cos_ref, sin_ref, out_ref, bias_ref, dk_ref, dv_ref
):
    size = cos_ref.shape[1]
    scale = size ** (-0.5)
    dk_ref[...] = jnp.zeros_like(dk_ref)
    dv_ref[...] = jnp.zeros_like(dv_ref)
    bias = jnp.zeros((1, size), WIDE)
    for start in range(0, q_ref.shape[0], QUERY_ROWS):
        end = start + QUERY_ROWS
        queries, grads = q_ref[start:end], grad_ref[start:end]
        probs = probabilities(queries, k_ref[:end], start, scale)
        grad_probs = dot_rows(grads, v_ref[:end])
        inner = jnp.sum(probs * grad_probs, axis=-1, keepdims=True)
        grad_scores = low(probs * (grad_probs - inner))
        grad_queries = jnp.dot(grad_scores, k_ref[:end], preferred_element_type=WIDE) * scale
        grad_queries = low(turn(grad_queries, cos_ref[start:end], -sin_ref[start:end]))
        out_ref[start:end, :size] = grad_queries
        bias = bias + jnp.sum(wide(grad_queries), axis=0, keepdims=True)
        dk_ref[:end] += dot_columns(grad_scores, queries) * scale
        dv_ref[:end] += dot_columns(low(probs), grads)
    bias_ref[:, :size] = bias
    grad_keys = low(turn(dk_ref[...], cos_ref[...], -sin_ref[...]))
    out_ref[:, size : 2 * size] = grad_keys
    bias_ref[:, size : 2 * size] = jnp.sum(wide(grad_keys), axis=0, keepdims=True)
    grad_values = low(dv_ref[...])
    out_ref[:, 2 * size :] = grad_values
    bias_ref[:, 2 * size :] = jnp.sum(wide(grad_values), axis=0, keepdims=True)


def attend(proj, cosine, sine):
    rows, size = cosine.shape
    one = jax.ShapeDtypeStruct((rows, size), LOW)
    return pl.pallas_call(
        attend_kernel,
        out_shape=(one, one, one, one),
        compiler_params=pltpu.CompilerParams(vmem_limit_bytes=VMEM_BYTES),
        name="attend",
    )(proj, cosine, sine)


def attend_back(queries, keys, values, grads, cosine, sine):
    rows, size = cosine.shape
    return pl.pallas_call(
        attend_back_kernel,
        out_shape=(
            jax.ShapeDtypeStruct((rows, 3 * size), LOW),
            jax.ShapeDtypeStruct((1, 3 * size), WIDE),
        ),
        scratch_shapes=[pltpu.VMEM((rows, size), WIDE), pltpu.VMEM((rows, size), WIDE)],
        compiler_params=pltpu.CompilerParams(vmem_limit_bytes=VMEM_BYTES),
        name="attend_back",
    )(queries, keys, values, grads, cosine, sine)


def gated_unit(normed, grad_top, weight_gate, weight_up, weight_down, scale):
    gate = jnp.dot(normed, weight_gate, preferred_element_type=WIDE)
    upper = jnp.dot(normed, weight_up, preferred_element_type=WIDE)
    back = jnp.dot(grad_top, weight_down, preferred_element_type=WIDE)
    sigmoid = jax.nn.sigmoid(gate)
    silu = gate * sigmoid
    hidden = silu * upper
    hidden_scaled = low(hidden * scale)
    grad_scale = jnp.sum(hidden * back, axis=-1, keepdims=True)
    grad_hidden = back * scale
    grad_gate = low(grad_hidden * upper * (sigmoid * (1.0 + gate * (1.0 - sigmoid))))
    grad_up = low(grad_hidden * silu)
    mixed = dot_rows(hidden_scaled, weight_down)
    grad_normed = dot_rows(grad_gate, weight_gate) + dot_rows(grad_up, weight_up)
    return (
        mixed,
        grad_normed,
        grad_scale,
        low(dot_columns(normed, grad_gate)),
        low(dot_columns(normed, grad_up)),
        low(dot_columns(grad_top, hidden_scaled)),
    )


def body(
    inputs,
    lengths,
    routes,
    norm_gains,
    w_qkv,
    b_qkv,
    w_o,
    w_router,
    w_sgate,
    w_sgu,
    w_sdown,
    w_egu,
    w_edown,
    grad_out,
):
    rows, width = inputs.shape
    shard = w_qkv.shape[0]
    experts = w_egu.shape[1]
    heads, bias_part = b_qkv.shape[1], b_qkv.shape[2]
    head_size = bias_part * 8
    expert_units = w_edown.shape[2]
    shared_units = w_sdown.shape[1] // 8
    group, here = lax.axis_index("fsdp"), lax.axis_index("ctx")
    places = here * rows + jnp.arange(rows, dtype=jnp.int32)
    length_here = lax.dynamic_index_in_dim(lengths, group, 0, keepdims=False)
    valid = (places < length_here).astype(WIDE)[:, None]
    experts_range = jnp.arange(experts, dtype=jnp.int32)
    chosen = (
        jnp.any(routes[:, :, None] == experts_range[None, None, :], axis=1).astype(WIDE) * valid
    )

    bias_here = lax.dynamic_slice(b_qkv, (0, here, 0), (3, 1, bias_part)).reshape(3 * bias_part)
    bias_column = jnp.pad(bias_here, (0, shard - 3 * bias_part))[:, None]
    small = jnp.concatenate(
        [norm_gains.T, w_sgate[:, None], w_router, bias_column], axis=1
    )
    small = jnp.pad(small, ((0, 0), (0, 128 - small.shape[1])))
    qkv_here = lax.dynamic_slice(
        w_qkv, (0, 0, here * head_size), (shard, 3, head_size)
    ).reshape(shard, 3 * head_size)
    first_pack = lax.all_gather(
        jnp.concatenate([qkv_here, small], axis=1), "fsdp", axis=0, tiled=True
    )
    weight_qkv, small_all = first_pack[:, : 3 * head_size], first_pack[:, 3 * head_size :]
    gain_first, gain_second = wide(small_all[:, 0]), wide(small_all[:, 1])
    weight_sgate, weight_router = small_all[:, 2:3], small_all[:, 3 : 3 + experts]
    bias_all = small_all[:, 3 + experts].reshape(8, shard)[:, : 3 * bias_part]
    bias_all = wide(bias_all.reshape(8, 3, bias_part).transpose(1, 0, 2).reshape(3 * head_size))
    weight_out = lax.all_gather(w_o, "fsdp", axis=0, tiled=True)
    shared_start = here * shared_units
    shared_gu = lax.dynamic_slice(w_sgu, (0, 0, shared_start), (shard, 2, shared_units))
    shared_down = lax.dynamic_slice(w_sdown, (0, shared_start), (shard, shared_units))
    expert_gu = lax.dynamic_slice(w_egu, (0, here, 0, 0), (shard, 1, 2, expert_units))
    expert_down = lax.dynamic_slice(w_edown, (0, here, 0), (shard, 1, expert_units))
    second_pack = lax.all_gather(
        jnp.concatenate(
            [
                expert_gu.reshape(shard, 2 * expert_units),
                expert_down.reshape(shard, expert_units),
                shared_gu.reshape(shard, 2 * shared_units),
                shared_down,
            ],
            axis=1,
        ),
        "fsdp",
        axis=0,
        tiled=True,
    )
    expert_columns = second_pack[:, : 3 * expert_units]
    shared_columns = second_pack[:, 3 * expert_units :]
    weight_qkv_all = lax.all_gather(w_qkv, "fsdp", axis=0, tiled=True)

    cosine, sine = rotary_tables(rows * 8, head_size)
    grad_own = low(wide(grad_out) * valid)
    hidden_in = wide(inputs)
    hidden_all = in_order(gather_relative(inputs)).reshape(rows * 8, width)
    hidden_wide = wide(hidden_all)
    normed_first = low(hidden_wide * inverse_rms(hidden_wide) * gain_first)
    proj = jnp.dot(normed_first, weight_qkv, preferred_element_type=WIDE) + bias_all
    queries, keys, values, attended = attend(proj, cosine, sine)
    attended_own = lax.all_to_all(attended, "ctx", 0, 1, tiled=True)
    grad_pack = jnp.concatenate(
        [grad_own, jnp.pad(low(chosen), ((0, 0), (0, 128 - experts)))], axis=1
    )
    grad_all = jnp.concatenate(gather_relative(grad_pack), axis=0)
    grad_top_all, chosen_all = grad_all[:, :width], wide(grad_all[:, width : width + experts])
    branch = add_halves(dot_rows(attended_own, weight_out))
    middle = hidden_in + branch
    factor_second = inverse_rms(middle)
    normed_own = low(middle * factor_second * gain_second)

    normed_all = jnp.concatenate(gather_relative(normed_own), axis=0)
    logits = jnp.dot(normed_all, weight_router, preferred_element_type=WIDE)
    router_probs = jax.nn.softmax(logits, axis=-1)
    shared_gate = jax.nn.sigmoid(jnp.dot(normed_all, weight_sgate, preferred_element_type=WIDE))
    mine = (experts_range == here).astype(WIDE)[None, :]
    combine = jnp.sum(chosen_all * router_probs * mine, axis=-1, keepdims=True)
    expert = gated_unit(
        normed_all,
        grad_top_all,
        expert_columns[:, :expert_units],
        expert_columns[:, expert_units : 2 * expert_units],
        expert_columns[:, 2 * expert_units :],
        combine,
    )
    shared = gated_unit(
        normed_all,
        grad_top_all,
        shared_columns[:, :shared_units],
        shared_columns[:, shared_units : 2 * shared_units],
        shared_columns[:, 2 * shared_units :],
        shared_gate,
    )
    mixed_all = expert[0] + shared[0]
    scales_all = jnp.concatenate([expert[2] * mine, shared[2]], axis=1)
    scales_all = jnp.pad(scales_all, ((0, 0), (0, 128 - experts - 1)))
    grad_normed_all = jnp.concatenate([expert[1] + shared[1], scales_all], axis=1)

    def split(values):
        return [values[index * rows : (index + 1) * rows] for index in range(8)]

    grad_sum = add_halves(scatter_relative(split(grad_normed_all)))
    mlp_grads = lax.psum_scatter(
        jnp.concatenate(list(expert[3:]) + list(shared[3:]), axis=1),
        "fsdp",
        scatter_dimension=0,
        tiled=True,
    )
    mixed = add_halves(scatter_relative(split(mixed_all)))
    result = low(valid * (middle + mixed))

    probs_own, gate_own = router_probs[:rows], shared_gate[:rows]
    grad_normed, grad_combine = grad_sum[:, :width], grad_sum[:, width : width + experts]
    grad_gate = grad_sum[:, width + experts : width + experts + 1]
    picked = grad_combine * chosen
    grad_logits = low(
        probs_own * (picked - jnp.sum(picked * probs_own, axis=-1, keepdims=True))
    )
    grad_gate_logit = low(grad_gate * gate_own * (1.0 - gate_own))
    both = jnp.concatenate([grad_logits, grad_gate_logit], axis=1)
    both_weights = jnp.concatenate([weight_router, weight_sgate], axis=1)
    grad_normed = grad_normed + dot_rows(both, both_weights)
    grad_both = dot_columns(normed_own, both)
    grad_top = wide(grad_own)
    grad_gain_second = jnp.sum(grad_normed * middle * factor_second, axis=0)
    weighted = grad_normed * gain_second
    inner = jnp.mean(weighted * middle, axis=-1, keepdims=True)
    grad_middle = grad_top + weighted * factor_second - middle * factor_second**3 * inner
    grad_branch = low(grad_middle)

    grad_attended = low(jnp.dot(grad_branch, weight_out, preferred_element_type=WIDE))
    grad_heads = lax.all_to_all(
        grad_attended.reshape(rows, heads, head_size).transpose(1, 0, 2), "ctx", 0, 0, tiled=True
    ).reshape(rows * 8, head_size)
    grad_proj, grad_bias = attend_back(queries, keys, values, grad_heads, cosine, sine)
    proj_own = lax.all_to_all(grad_proj.reshape(8, rows, 3 * head_size), "ctx", 0, 0, tiled=True)
    proj_own = proj_own.reshape(8, rows, 3, head_size).transpose(1, 2, 0, 3)
    grad_first = lax.dot_general(
        proj_own.reshape(rows, 3 * heads * head_size),
        weight_qkv_all.reshape(width, 3 * heads * head_size),
        (((1,), (1,)), ((), ())),
        preferred_element_type=WIDE,
    )
    grad_first = add_halves(grad_first)
    factor_first = inverse_rms(hidden_in)
    weighted = grad_first * gain_first
    inner = jnp.mean(weighted * hidden_in, axis=-1, keepdims=True)
    grad_input = grad_middle + weighted * factor_first - hidden_in * factor_first**3 * inner

    grad_out_part = lax.psum_scatter(
        low(dot_columns(grad_branch, attended_own)), "fsdp", scatter_dimension=0, tiled=True
    )
    grad_w_o_here = scatter_relative(
        [
            lax.dynamic_slice(grad_out_part, (0, place * head_size), (shard, head_size))
            for place in relative_places()
        ]
    )
    grad_qkv_here = low(dot_columns(normed_first, grad_proj))
    bias_rows = grad_bias.reshape(3, 8, bias_part).transpose(1, 0, 2).reshape(8, 3 * bias_part)
    bias_rows = jnp.pad(bias_rows, ((0, 0), (0, shard - 3 * bias_part))).reshape(width, 1)
    small_grads = low(jnp.concatenate([grad_both, grad_gain_second[:, None], bias_rows], axis=1))
    small_grads = jnp.pad(small_grads, ((0, 0), (0, 128 - small_grads.shape[1])))
    last_pack = lax.psum_scatter(
        jnp.concatenate([grad_qkv_here, small_grads], axis=1),
        "fsdp",
        scatter_dimension=0,
        tiled=True,
    )
    mlp_all = in_order(gather_relative(mlp_grads))
    last_all = in_order(
        gather_relative(jnp.concatenate([last_pack, low(grad_w_o_here)], axis=1))
    )
    expert_gu_all = wide(mlp_all[:, :, : 2 * expert_units])
    grad_w_egu = expert_gu_all.reshape(8, shard, 2, expert_units).transpose(1, 0, 2, 3)
    grad_w_edown = wide(mlp_all[:, :, 2 * expert_units : 3 * expert_units]).transpose(1, 0, 2)
    shared_gu_all = wide(mlp_all[:, :, 3 * expert_units : 3 * expert_units + 2 * shared_units])
    grad_w_sgu = (
        shared_gu_all.reshape(8, shard, 2, shared_units)
        .transpose(1, 2, 0, 3)
        .reshape(shard, 2, 8 * shared_units)
    )
    grad_w_sdown = (
        wide(mlp_all[:, :, 3 * expert_units + 2 * shared_units :])
        .transpose(1, 0, 2)
        .reshape(shard, 8 * shared_units)
    )
    qkv_size = 3 * head_size
    grad_w_qkv = (
        wide(last_all[:, :, :qkv_size])
        .reshape(8, shard, 3, head_size)
        .transpose(1, 2, 0, 3)
        .reshape(shard, 3, heads * head_size)
    )
    small_sums = wide(last_all[:, :, qkv_size : qkv_size + 128])
    grad_w_o = (
        wide(last_all[:, :, qkv_size + 128 :]).transpose(1, 0, 2).reshape(shard, heads * head_size)
    )
    summed = jnp.sum(small_sums[:, :, : experts + 2], axis=0)
    grad_b_qkv = (
        small_sums[:, : 3 * bias_part, experts + 2].reshape(8, 3, bias_part).transpose(1, 0, 2)
    )
    products = jnp.sum(grad_w_qkv * wide(w_qkv), axis=(1, 2))
    products = products + lax.ppermute(products, "tp", [(0, 1), (1, 0)])
    grad_gain_first = products / wide(norm_gains[0])
    return (
        result,
        low(grad_input),
        jnp.stack([grad_gain_first, summed[:, experts + 1]]),
        grad_w_qkv,
        grad_b_qkv,
        grad_w_o,
        summed[:, :experts],
        summed[:, experts],
        grad_w_sgu,
        grad_w_sdown,
        grad_w_egu,
        grad_w_edown,
    )


def solution(mesh):
    return jax.shard_map(
        body,
        mesh=mesh,
        in_specs=(
            P(("fsdp", "ctx"), None),
            P(),
            P(("fsdp", "ctx"), None),
            P(None, "fsdp"),
            P("fsdp", None, "tp"),
            P(None, "tp", "fsdp"),
            P("fsdp", "tp"),
            P("fsdp", None),
            P("fsdp"),
            P("fsdp", None, "tp"),
            P("fsdp", "tp"),
            P("fsdp", None, None, "tp"),
            P("fsdp", None, "tp"),
            P(("fsdp", "ctx"), None),
        ),
        out_specs=(
            P(("fsdp", "ctx"), None),
            P(("fsdp", "ctx"), None),
            P(None, "fsdp"),
            P("fsdp", None, "tp"),
            P(None, "tp", "fsdp"),
            P("fsdp", "tp"),
            P("fsdp", None),
            P("fsdp"),
            P("fsdp", None, "tp"),
            P("fsdp", "tp"),
            P("fsdp", None, None, "tp"),
            P("fsdp", None, "tp"),
        ),
        check_vma=False,
    )
```

```python
import jax
import jax.numpy as jnp
import numpy as np
from jax import lax
from jax.experimental import pallas as pl
from jax.experimental.pallas import tpu as pltpu
from jax.sharding import PartitionSpec as P

EPSILON = 1e-06
ROPE_BASE = 1000000.0
MASKED_SCORE = -1e30
LOW = jnp.bfloat16
WIDE = jnp.float32
VMEM_BYTES = 56 * 1024 * 1024


def low(values):
    return values.astype(LOW)


def wide(values):
    return values.astype(WIDE)


def rotary_tables(row_count, head_size):
    middle = head_size // 2
    powers = -(np.arange(middle, dtype=np.float32) * np.float32(2.0)) / np.float32(head_size)
    inverse = np.power(np.float32(ROPE_BASE), powers).astype(np.float32)
    places = np.arange(row_count, dtype=np.float32)
    angles = (places[:, None] * inverse[None, :]).astype(np.float32)
    cosine, sine = np.cos(angles), np.sin(angles)
    return (
        jnp.asarray(np.concatenate([cosine, cosine], axis=-1)),
        jnp.asarray(np.concatenate([-sine, sine], axis=-1)),
    )


def inverse_rms(values):
    return lax.rsqrt(jnp.mean(values * values, axis=-1, keepdims=True) + EPSILON)


def ring(step):
    return [(i, (i + step) % 8) for i in range(8)]


PAIR = [(i, i ^ 1) for i in range(8)]


def up(values):
    return lax.ppermute(values, "ctx", ring(2))


def down(values):
    return lax.ppermute(values, "ctx", ring(-2))


def swap(values):
    return lax.ppermute(values, "ctx", PAIR)


def relative_places():
    here = lax.axis_index("ctx")
    return [(here + step) % 8 for step in (0, 6, 2, 4)] + [
        ((here ^ 1) + step) % 8 for step in (0, 6, 2, 4)
    ]


def across(values):
    return lax.ppermute(values, "ctx", ring(4))


def gather_first(block):
    return up(block), down(block), swap(block), across(block)


def gather_second(first):
    _, _, pair, opposite = first
    return up(pair), down(pair), swap(opposite)


def gather_blocks(block, first, second):
    left, right, pair, opposite = first
    return [block, left, right, opposite, pair, *second]


def gather_relative(block):
    first = gather_first(block)
    return gather_blocks(block, first, gather_second(first))


def large_first(block):
    return up(block), down(block), swap(block)


def large_second(first):
    left, right, pair = first
    half = left.shape[0] // 2
    return up(left[:half]), down(right[half:]), up(pair), down(pair)


def large_third(second):
    _, _, pair_left, pair_right = second
    half = pair_left.shape[0] // 2
    return up(pair_left[:half]), down(pair_right[half:])


def large_blocks(block, first, second, third):
    left, right, pair = first
    opposite = jnp.concatenate(second[:2], axis=0)
    pair_opposite = jnp.concatenate(third, axis=0)
    return [block, left, right, opposite, pair, second[2], second[3], pair_opposite]


def scatter_first(blocks):
    _, _, _, _, _, pair_left, pair_right, pair_opposite = blocks
    return swap(low(pair_opposite)), up(low(pair_right)), down(low(pair_left))


def scatter_second(blocks, first):
    _, left, right, opposite, pair, _, _, _ = blocks
    from_pair, pair_up, pair_down = first
    return (
        across(low(wide(opposite) + wide(from_pair))),
        swap(low(wide(pair) + wide(pair_up) + wide(pair_down))),
        up(low(right)),
        down(low(left)),
    )


def scatter_sum(own, second):
    far, crossing, last_up, last_down = second
    return wide(own) + wide(far) + wide(crossing) + wide(last_up) + wide(last_down)


def scatter_relative(blocks):
    return scatter_sum(blocks[0], scatter_second(blocks, scatter_first(blocks)))


def add_halves(values):
    mine = low(values)
    return wide(mine) + wide(lax.ppermute(mine, "tp", [(0, 1), (1, 0)]))


QUERY_ROWS = 256


def estimate(flops, bytes_accessed):
    return pl.CostEstimate(
        flops=flops // 1000, bytes_accessed=bytes_accessed // 1000, transcendentals=0
    )


def params():
    return pltpu.CompilerParams(vmem_limit_bytes=VMEM_BYTES)


def turn(values, cosine, sine):
    return values * cosine + pltpu.roll(values, values.shape[-1] // 2, 1) * sine


def dot_plain(left, right):
    return jnp.dot(left, right, preferred_element_type=WIDE)


def dot_rows(left, right):
    return lax.dot_general(left, right, (((1,), (1,)), ((), ())), preferred_element_type=WIDE)


def dot_columns(left, right):
    return lax.dot_general(left, right, (((0,), (0,)), ((), ())), preferred_element_type=WIDE)


def probabilities(queries, keys, start, scale):
    scores = dot_rows(queries, keys) * scale
    rows = start + lax.broadcasted_iota(jnp.int32, scores.shape, 0)
    columns = lax.broadcasted_iota(jnp.int32, scores.shape, 1)
    scores = jnp.where(columns <= rows, scores, MASKED_SCORE)
    expons = jnp.exp(scores - jnp.max(scores, axis=-1, keepdims=True))
    return expons / jnp.sum(expons, axis=-1, keepdims=True)


def block_rows(place, rows):
    return pl.ds(pl.multiple_of(place * rows, rows), rows)


def attend_kernel(places_ref, *refs):
    blocks = refs[:8]
    weight_ref, gain_ref, bias_ref, cos_ref, sin_ref = refs[8:13]
    q_ref, k_ref, v_ref, out_ref, normed_ref = refs[13:]
    size = cos_ref.shape[1]
    scale = size ** (-0.5)
    gain = gain_ref[...]
    for index, block in enumerate(blocks):
        values = wide(block[...])
        normed = low(values * inverse_rms(values) * gain)
        normed_ref[block_rows(places_ref[index], block.shape[0]), :] = normed
    for start in range(0, q_ref.shape[0], QUERY_ROWS):
        end = start + QUERY_ROWS
        proj = dot_plain(normed_ref[start:end], weight_ref[:, : 3 * size]) + bias_ref[...]
        cosine, sine = cos_ref[start:end], sin_ref[start:end]
        q_ref[start:end] = low(turn(proj[:, :size], cosine, sine))
        k_ref[start:end] = low(turn(proj[:, size : 2 * size], cosine, sine))
        v_ref[start:end] = low(proj[:, 2 * size :])
    for start in range(0, q_ref.shape[0], QUERY_ROWS):
        end = start + QUERY_ROWS
        probs = low(probabilities(q_ref[start:end], k_ref[:end], start, scale))
        out_ref[start:end] = low(dot_plain(probs, v_ref[:end]))


def attend(places, blocks, pack, gain, bias, cosine, sine):
    rows, size = cosine.shape
    width = blocks[0].shape[1]
    one = jax.ShapeDtypeStruct((rows, size), LOW)
    whole = pl.BlockSpec(memory_space=pltpu.VMEM)
    part = pl.BlockSpec((width, 512), lambda step: (0, 2))
    whole_of = lambda shape: pl.BlockSpec(shape, lambda step: (0, 0))
    return pl.pallas_call(
        attend_kernel,
        grid=(1,),
        in_specs=[pl.BlockSpec(memory_space=pltpu.SMEM)]
        + [whole_of(block.shape) for block in blocks]
        + [part]
        + [whole_of(value.shape) for value in (gain, bias, cosine, sine)],
        out_specs=[whole_of((rows, size))] * 4 + [whole_of((rows, width))],
        out_shape=(one, one, one, one, jax.ShapeDtypeStruct((rows, width), LOW)),
        compiler_params=params(),
        cost_estimate=estimate(9_000_000_000, 12_000_000),
        name="attend",
    )(places, *blocks, pack, gain, bias, cosine, sine)


def attend_back_kernel(
    q_ref, k_ref, v_ref, grad_ref, cos_ref, sin_ref, out_ref, bias_ref, dk_ref, dv_ref
):
    size = cos_ref.shape[1]
    scale = size ** (-0.5)
    dk_ref[...] = jnp.zeros_like(dk_ref)
    dv_ref[...] = jnp.zeros_like(dv_ref)
    bias = jnp.zeros((1, size), WIDE)
    for start in range(0, q_ref.shape[0], QUERY_ROWS):
        end = start + QUERY_ROWS
        queries, grads = q_ref[start:end], grad_ref[start:end]
        probs = probabilities(queries, k_ref[:end], start, scale)
        grad_probs = dot_rows(grads, v_ref[:end])
        inner = jnp.sum(probs * grad_probs, axis=-1, keepdims=True)
        grad_scores = low(probs * (grad_probs - inner))
        grad_queries = dot_plain(grad_scores, k_ref[:end]) * scale
        grad_queries = low(turn(grad_queries, cos_ref[start:end], -sin_ref[start:end]))
        out_ref[start:end, :size] = grad_queries
        bias = bias + jnp.sum(wide(grad_queries), axis=0, keepdims=True)
        dk_ref[:end] += dot_columns(grad_scores, queries) * scale
        dv_ref[:end] += dot_columns(low(probs), grads)
    bias_ref[:, :size] = bias
    grad_keys = low(turn(dk_ref[...], cos_ref[...], -sin_ref[...]))
    out_ref[:, size : 2 * size] = grad_keys
    bias_ref[:, size : 2 * size] = jnp.sum(wide(grad_keys), axis=0, keepdims=True)
    grad_values = low(dv_ref[...])
    out_ref[:, 2 * size :] = grad_values
    bias_ref[:, 2 * size :] = jnp.sum(wide(grad_values), axis=0, keepdims=True)


def attend_back(queries, keys, values, grads, cosine, sine):
    rows, size = cosine.shape
    return pl.pallas_call(
        attend_back_kernel,
        out_shape=(
            jax.ShapeDtypeStruct((rows, 3 * size), LOW),
            jax.ShapeDtypeStruct((1, 3 * size), WIDE),
        ),
        scratch_shapes=[pltpu.VMEM((rows, size), WIDE), pltpu.VMEM((rows, size), WIDE)],
        compiler_params=params(),
        cost_estimate=estimate(7_000_000_000, 6_000_000),
        name="attend_back",
    )(queries, keys, values, grads, cosine, sine)


UNIT_ROWS = 16


def units_kernel(*refs):
    x_hbm, g_hbm = refs[:4], refs[4:8]
    small_ref, mine_ref, weight_hbm = refs[8:11]
    d_hbm, back_hbm, hidden_hbm = refs[11:15], refs[15], refs[16]
    weight_ref, x_ref, g_ref, tail_ref, gate_ref, up_ref, down_ref = refs[17:24]
    back_ref, hidden_ref, turned_ref, flat_ref, d_ref, sems = refs[24:]
    units, tokens = hidden_ref.shape
    rows, width = x_hbm[0].shape
    expert_units = units * 2 // 3
    count = 0
    started = {}

    def start(name, source, target):
        nonlocal count
        copy = pltpu.make_async_copy(source, target, sems.at[count])
        copy.start()
        count += 1
        started.setdefault(name, []).append(copy)

    def finish(name):
        for copy in started[name]:
            copy.wait()

    def start_weights(part):
        group = pl.ds(part * units, units)
        for index in range(8):
            columns = pl.ds(index * (width // 8), width // 8)
            start(part, weight_hbm.at[index, group, :], weight_ref.at[group, columns])

    block = lambda index: pl.ds(index * rows, rows)
    for index in range(4):
        start("x", x_hbm[index], x_ref.at[block(index)])
    start_weights(0)
    start_weights(1)
    for index in range(4):
        start("tail", g_hbm[index].at[:, pl.ds(width, 128)], tail_ref.at[block(index)])
        start("g", g_hbm[index].at[:, pl.ds(0, width)], g_ref.at[block(index)])
    start_weights(2)
    finish("x")
    logits = dot_rows(small_ref[...], x_ref[...])
    places = lax.broadcasted_iota(jnp.int32, logits.shape, 0)
    routed = jnp.where(places < 8, logits, MASKED_SCORE)
    expons = jnp.exp(routed - jnp.max(routed, axis=0, keepdims=True))
    probs = expons / jnp.sum(expons, axis=0, keepdims=True)
    shared_gate = jax.nn.sigmoid(
        jnp.sum(jnp.where(places == 8, logits, 0.0), axis=0, keepdims=True)
    )
    for part, (target, source) in enumerate(((gate_ref, x_ref), (up_ref, x_ref), (down_ref, g_ref))):
        if part == 2:
            finish("g")
        finish(part)
        target[...] = dot_rows(weight_ref[part * units : (part + 1) * units], source[...])
    finish("tail")
    chosen = wide(tail_ref[...]).T[: places.shape[0]]
    mine = mine_ref[...]
    combine = jnp.sum(probs * chosen * mine, axis=0, keepdims=True)

    def unit_rows(scale):
        def step(index, total):
            chunk = pl.ds(pl.multiple_of(index * UNIT_ROWS, UNIT_ROWS), UNIT_ROWS)
            after = pl.ds(pl.multiple_of(units + index * UNIT_ROWS, UNIT_ROWS), UNIT_ROWS)
            gate, upper, back = gate_ref[chunk, :], up_ref[chunk, :], down_ref[chunk, :]
            sigmoid = jax.nn.sigmoid(gate)
            silu = gate * sigmoid
            hidden = silu * upper
            hidden_ref[chunk, :] = low(hidden * scale)
            grad_hidden = back * scale
            back_ref[chunk, :] = low(grad_hidden * upper * (sigmoid + silu * (1.0 - sigmoid)))
            back_ref[after, :] = low(grad_hidden * silu)
            return total + hidden * back

        return step

    zeros = jnp.zeros((UNIT_ROWS, tokens), WIDE)
    middle, last = expert_units // UNIT_ROWS, units // UNIT_ROWS
    expert_sum = lax.fori_loop(0, middle, unit_rows(combine), zeros)
    shared_sum = lax.fori_loop(middle, last, unit_rows(shared_gate), zeros)
    start("out", hidden_ref, hidden_hbm)
    start("out", back_ref, back_hbm)
    expert_sum = jnp.sum(expert_sum, axis=0, keepdims=True)
    shared_sum = jnp.sum(shared_sum, axis=0, keepdims=True)
    sums = mine * expert_sum + jnp.where(places == 8, shared_sum, 0.0)
    sums = jnp.concatenate([sums, jnp.zeros((128 - sums.shape[0], tokens), WIDE)], axis=0)
    d_ref[:, width : width + 128] = low(sums.T)
    turned_ref[...] = back_ref[...].T
    step = width // 4

    def send(begin, size):
        for index in range(4):
            source = d_ref.at[block(index), pl.ds(begin, size)]
            start("out", source, d_hbm[index].at[:, pl.ds(begin, size)])

    for part in range(4):
        columns = slice(part * step, (part + 1) * step)
        d_ref[:, columns] = low(dot_plain(turned_ref[...], weight_ref[: 2 * units, columns]))
        send(part * step, step if part < 3 else step + 128)
    flat_ref[...] = hidden_ref[...].T
    for part in range(4):
        columns = slice(part * step, (part + 1) * step)
        begin = width + 128 + part * step
        d_ref[:, begin : begin + step] = low(
            dot_plain(flat_ref[...], weight_ref[2 * units :, columns])
        )
        send(begin, step)
    finish("out")


def units_forward_back(x_blocks, g_blocks, small_rows, mine, weights):
    rows, width = x_blocks[0].shape
    tokens = 4 * rows
    units = weights.shape[1] // 3
    vmem = pl.BlockSpec(memory_space=pltpu.VMEM)
    anywhere = pl.BlockSpec(memory_space=pl.ANY)
    return pl.pallas_call(
        units_kernel,
        in_specs=[anywhere] * 8 + [vmem] * 2 + [anywhere],
        out_specs=[anywhere] * 6,
        out_shape=[jax.ShapeDtypeStruct((rows, 2 * width + 128), LOW)] * 4
        + [
            jax.ShapeDtypeStruct((2 * units, tokens), LOW),
            jax.ShapeDtypeStruct((units, tokens), LOW),
        ],
        scratch_shapes=[
            pltpu.VMEM((3 * units, width), LOW),
            pltpu.VMEM((tokens, width), LOW),
            pltpu.VMEM((tokens, width), LOW),
            pltpu.VMEM((tokens, 128), LOW),
            pltpu.VMEM((units, tokens), WIDE),
            pltpu.VMEM((units, tokens), WIDE),
            pltpu.VMEM((units, tokens), WIDE),
            pltpu.VMEM((2 * units, tokens), LOW),
            pltpu.VMEM((units, tokens), LOW),
            pltpu.VMEM((tokens, 2 * units), LOW),
            pltpu.VMEM((tokens, units), LOW),
            pltpu.VMEM((tokens, 2 * width + 128), LOW),
            pltpu.SemaphoreType.DMA((70,)),
        ],
        compiler_params=params(),
        cost_estimate=estimate(11_000_000_000, 20_000_000),
        name="units",
    )(*x_blocks, *g_blocks, small_rows, mine, weights)


def outer_kernel(*refs):
    back_refs, hidden_refs, x_refs, g_refs, out_ref = (
        refs[:2],
        refs[2:4],
        refs[4:12],
        refs[12:20],
        refs[20],
    )
    units = hidden_refs[0].shape[0]

    def product(lefts, rights):
        halves = [
            jnp.concatenate([ref[...] for ref in rights[half : half + 4]], axis=0)
            for half in (0, 4)
        ]
        return low(dot_plain(lefts[0][...], halves[0]) + dot_plain(lefts[1][...], halves[1]))

    back, hidden = product(back_refs, x_refs), product(hidden_refs, g_refs)
    for index in range(out_ref.shape[0]):
        columns = slice(index * 256, (index + 1) * 256)
        out_ref[index, : 2 * units] = back[:, columns]
        out_ref[index, 2 * units :] = hidden[:, columns]


def outer_products(backs, hiddens, x_blocks, g_blocks):
    units, tokens = hiddens[0].shape
    rows = x_blocks[0].shape[0]
    whole = lambda value: pl.BlockSpec(value.shape, lambda step: (0, 0))
    return pl.pallas_call(
        outer_kernel,
        grid=(4,),
        in_specs=[whole(value) for value in (*backs, *hiddens)]
        + [pl.BlockSpec((rows, 512), lambda step: (0, step))] * 16,
        out_specs=pl.BlockSpec((2, 3 * units, 256), lambda step: (step, 0, 0)),
        out_shape=jax.ShapeDtypeStruct((8, 3 * units, 256), LOW),
        compiler_params=params(),
        cost_estimate=estimate(units * 2 * 1024 * 2048, 10_000_000),
        name="outer",
    )(*backs, *hiddens, *x_blocks, *g_blocks)


def pack_kernel(here_ref, qkv_ref, out_weight_ref, small_ref, out_ref):
    width, size = out_weight_ref.shape[1], qkv_ref.shape[2]
    out_ref[:, :width] = out_weight_ref[...]
    for index in range(3):
        out_ref[:, width + index * size : width + (index + 1) * size] = qkv_ref[index]
    out_ref[:, width + 3 * size :] = jnp.zeros_like(out_ref[:, width + 3 * size :])
    out_ref[: small_ref.shape[0], width + 3 * size :] = small_ref[...]


def pack_first(here, qkv, out_weight, small):
    shard, width = out_weight.shape
    return pl.pallas_call(
        pack_kernel,
        grid_spec=pltpu.PrefetchScalarGridSpec(
            num_scalar_prefetch=1,
            grid=(1,),
            in_specs=[
                pl.BlockSpec((3, shard, 128), lambda step, here_ref: (0, 0, here_ref[0])),
                pl.BlockSpec((shard, width), lambda step, here_ref: (0, 0)),
                pl.BlockSpec(small.shape, lambda step, here_ref: (0, 0)),
            ],
            out_specs=pl.BlockSpec((shard, width + 512), lambda step, here_ref: (0, 0)),
        ),
        out_shape=jax.ShapeDtypeStruct((shard, width + 512), LOW),
        cost_estimate=estimate(1000, 1000),
        name="pack",
    )(here, qkv, out_weight, small)


def branch_kernel(left_ref, weight_ref, out_ref):
    out_ref[...] = low(dot_rows(left_ref[...], weight_ref[...]))


def branch_part(attended, pack):
    rows, units = attended.shape
    width = pack.shape[0]
    return pl.pallas_call(
        branch_kernel,
        grid=(4,),
        in_specs=[
            pl.BlockSpec((rows, units), lambda step: (0, 0)),
            pl.BlockSpec((width // 4, units), lambda step: (step, 0)),
        ],
        out_specs=pl.BlockSpec((rows, width // 4), lambda step: (0, step)),
        out_shape=jax.ShapeDtypeStruct((rows, width), LOW),
        cost_estimate=estimate(600_000_000, 5_000_000),
        name="branch",
    )(attended, pack)


def branch_back_kernel(left_ref, weight_ref, out_ref):
    out_ref[...] = low(dot_plain(left_ref[...], weight_ref[...]))


def branch_back(grads, pack, units):
    rows, width = grads.shape
    return pl.pallas_call(
        branch_back_kernel,
        grid=(4,),
        in_specs=[
            pl.BlockSpec((rows, width), lambda step: (0, 0)),
            pl.BlockSpec((width, units // 4), lambda step: (0, step)),
        ],
        out_specs=pl.BlockSpec((rows, units // 4), lambda step: (0, step)),
        out_shape=jax.ShapeDtypeStruct((rows, units), LOW),
        cost_estimate=estimate(600_000_000, 5_000_000),
        name="branch_back",
    )(grads, pack)


def first_back_kernel(left_ref, weight_ref, out_ref):
    total = dot_rows(left_ref[0], weight_ref[0, 0])
    for part in (1, 2):
        total = total + dot_rows(left_ref[part], weight_ref[0, part])
    out_ref[...] = low(total)


def first_back(grads, weights):
    parts, rows, units = grads.shape
    shards, _, shard, _ = weights.shape
    return pl.pallas_call(
        first_back_kernel,
        grid=(shards,),
        in_specs=[
            pl.BlockSpec((parts, rows, units), lambda step: (0, 0, 0)),
            pl.BlockSpec((1, parts, shard, units), lambda step: (step, 0, 0, 0)),
        ],
        out_specs=pl.BlockSpec((rows, shard), lambda step: (0, step)),
        out_shape=jax.ShapeDtypeStruct((rows, shards * shard), LOW),
        cost_estimate=estimate(1_700_000_000, 13_000_000),
        name="first_back",
    )(grads, weights)


def place_kernel(places_ref, *refs):
    blocks = refs[:8]
    qkv_ref, out_ref, small_ref = refs[8:]
    for index, block in enumerate(blocks):
        columns = block_rows(places_ref[index], 128)
        for part in range(3):
            qkv_ref[part, :, columns] = wide(block[:, part * 128 : (part + 1) * 128])
        out_ref[:, columns] = wide(block[:, 512:640])
        small_ref[places_ref[index]] = wide(block[:, 384:512])


def place_last(places, blocks):
    shard = blocks[0].shape[0]
    vmem = pl.BlockSpec(memory_space=pltpu.VMEM)
    return pl.pallas_call(
        place_kernel,
        in_specs=[pl.BlockSpec(memory_space=pltpu.SMEM)] + [vmem] * 8,
        out_specs=[vmem] * 3,
        out_shape=(
            jax.ShapeDtypeStruct((3, shard, 1024), WIDE),
            jax.ShapeDtypeStruct((shard, 1024), WIDE),
            jax.ShapeDtypeStruct((8, shard, 128), WIDE),
        ),
        compiler_params=params(),
        cost_estimate=estimate(1000, 1000),
        name="place",
    )(places, *blocks)


def place_units_kernel(places_ref, *refs):
    blocks, (gate_ref, down_ref, shared_ref) = refs[:4], refs[-3:]
    expert_units = down_ref.shape[1]
    units = blocks[0].shape[0] // 3
    step = pl.program_id(0)
    for index, block in enumerate(blocks):

        @pl.when(step == index)
        def _(block=block):
            for part in range(3):
                start = part * units
                expert = wide(block[start : start + expert_units])
                if part < 2:
                    gate_ref[0, part] = expert
                else:
                    down_ref[0] = expert
                shared_ref[part, 0] = block[start + expert_units : start + units]


def place_units(places, blocks, expert_units, earlier):
    total, shard = blocks[0].shape
    shared_units = total // 3 - expert_units
    outs = (
        jax.ShapeDtypeStruct((8, 2, expert_units, shard), WIDE),
        jax.ShapeDtypeStruct((8, expert_units, shard), WIDE),
        jax.ShapeDtypeStruct((3, 8, shared_units, shard), LOW),
    )
    anywhere = pl.BlockSpec(memory_space=pl.ANY)
    return pl.pallas_call(
        place_units_kernel,
        grid_spec=pltpu.PrefetchScalarGridSpec(
            num_scalar_prefetch=1,
            grid=(4,),
            in_specs=[pl.BlockSpec((total, shard), lambda step, places_ref: (0, 0))] * 4
            + [anywhere] * len(earlier),
            out_specs=[
                pl.BlockSpec(
                    (1, 2, expert_units, shard),
                    lambda step, places_ref: (places_ref[step], 0, 0, 0),
                ),
                pl.BlockSpec(
                    (1, expert_units, shard),
                    lambda step, places_ref: (places_ref[step], 0, 0),
                ),
                pl.BlockSpec(
                    (3, 1, shared_units, shard),
                    lambda step, places_ref: (0, places_ref[step], 0, 0),
                ),
            ],
        ),
        out_shape=outs,
        input_output_aliases={5 + index: index for index in range(len(earlier))},
        compiler_params=params(),
        cost_estimate=estimate(1000, 1000),
        name="place_units",
    )(places, *blocks, *earlier)


def flip_kernel(one_ref, in_ref, gate_ref, down_ref):
    for part in range(2):
        gate_ref[:, part, :] = dot_rows(one_ref[...], in_ref[part])
    down_ref[...] = dot_rows(one_ref[...], in_ref[2])


def flip(values):
    parts, units, shard = values.shape
    return pl.pallas_call(
        flip_kernel,
        grid=(2,),
        in_specs=[
            pl.BlockSpec((shard, shard), lambda step: (0, 0)),
            pl.BlockSpec((parts, units // 2, shard), lambda step: (0, step, 0)),
        ],
        out_specs=[
            pl.BlockSpec((shard, 2, units // 2), lambda step: (0, 0, step)),
            pl.BlockSpec((shard, units // 2), lambda step: (0, step)),
        ],
        out_shape=(
            jax.ShapeDtypeStruct((shard, 2, units), WIDE),
            jax.ShapeDtypeStruct((shard, units), WIDE),
        ),
        compiler_params=params(),
        cost_estimate=estimate(1000, 1000),
        name="flip",
    )(jnp.eye(shard, dtype=LOW), values)


def after(values, earlier):
    return lax.optimization_barrier((values, earlier))[0]


def body(
    inputs,
    lengths,
    routes,
    norm_gains,
    w_qkv,
    b_qkv,
    w_o,
    w_router,
    w_sgate,
    w_sgu,
    w_sdown,
    w_egu,
    w_edown,
    grad_out,
):
    rows, width = inputs.shape
    shard = w_qkv.shape[0]
    experts = w_egu.shape[1]
    heads, bias_part = b_qkv.shape[1], b_qkv.shape[2]
    head_size = bias_part * 8
    expert_units = w_edown.shape[2]
    shared_units = w_sdown.shape[1] // 8
    units = expert_units + shared_units
    group, here = lax.axis_index("fsdp"), lax.axis_index("ctx")
    places = here * rows + jnp.arange(rows, dtype=jnp.int32)
    length_here = lax.dynamic_index_in_dim(lengths, group, 0, keepdims=False)
    valid = (places < length_here).astype(WIDE)[:, None]
    experts_range = jnp.arange(experts, dtype=jnp.int32)
    chosen = (
        jnp.any(routes[:, :, None] == experts_range[None, None, :], axis=1).astype(WIDE) * valid
    )
    block_places = jnp.stack(relative_places()).astype(jnp.int32)

    bias_here = lax.dynamic_slice(b_qkv, (0, here, 0), (3, 1, bias_part)).reshape(1, 3 * bias_part)
    small = jnp.concatenate(
        [
            w_router.T,
            w_sgate[None],
            norm_gains,
            jnp.pad(bias_here, ((0, 0), (0, shard - 3 * bias_part))),
            jnp.zeros((4, shard), LOW),
        ],
        axis=0,
    )
    first_pack = lax.all_gather(
        pack_first(
            here.astype(jnp.int32).reshape(1),
            w_qkv.transpose(1, 0, 2),
            w_o,
            small.reshape(32, 128),
        ),
        "fsdp",
        axis=0,
        tiled=True,
    )
    small_all = first_pack[:, 1408:].reshape(8, shard, 128)[:, :32].reshape(8, 16, shard)
    small_all = small_all.transpose(1, 0, 2)
    bias_all = small_all[11, :, : 3 * bias_part].reshape(8, 3, bias_part)
    bias_all = wide(bias_all.transpose(1, 0, 2).reshape(1, 3 * head_size))
    small_all = small_all.reshape(16, width)
    gain_first, gain_second = wide(small_all[9]), wide(small_all[10])
    gate_rows = small_all[: experts + 1]
    small_rows = jnp.pad(gate_rows, ((0, 16 - experts - 1), (0, 0)))
    x_first = gather_first(inputs)
    x_second = gather_second(x_first)
    here_late = after(here, (x_first, x_second))
    shared_start = here_late * shared_units
    shared_gu = lax.dynamic_slice(w_sgu, (0, 0, shared_start), (shard, 2, shared_units))
    shared_gu = shared_gu.transpose(1, 2, 0)
    shared_down = lax.dynamic_slice(w_sdown, (0, shared_start), (shard, shared_units)).T
    expert_gu = lax.dynamic_index_in_dim(w_egu.transpose(1, 2, 3, 0), here_late, 0, keepdims=False)
    expert_down = lax.dynamic_index_in_dim(w_edown.transpose(1, 2, 0), here_late, 0, keepdims=False)
    unit_weights = lax.all_gather(
        jnp.concatenate(
            [expert_gu[0], shared_gu[0], expert_gu[1], shared_gu[1], expert_down, shared_down],
            axis=0,
        ),
        "fsdp",
        axis=0,
        tiled=False,
    )

    cosine, sine = rotary_tables(rows * 8, head_size)
    grad_own = low(wide(grad_out) * valid)
    hidden_in = wide(inputs)
    x_blocks = gather_blocks(inputs, x_first, x_second)
    grad_pack = jnp.concatenate(
        [grad_own, jnp.pad(low(chosen), ((0, 0), (0, 128 - experts)))], axis=1
    )
    grad_pack = after(grad_pack, x_second)
    g_first = gather_first(grad_pack)
    g_second = gather_second(g_first)
    g_blocks = gather_blocks(grad_pack, g_first, g_second)
    queries, keys, values, attended, normed_first = attend(
        block_places, x_blocks, first_pack, gain_first[None], bias_all, cosine, sine
    )
    attended_own = lax.all_to_all(attended, "ctx", 0, 1, tiled=True)
    branch = add_halves(after(branch_part(attended_own, first_pack), g_first))
    middle = hidden_in + branch
    factor_second = inverse_rms(middle)
    normed_own = low(middle * factor_second * gain_second)

    n_first = gather_first(normed_own)
    n_second = gather_second(n_first)
    n_blocks = gather_blocks(normed_own, n_first, n_second)
    mine = (jnp.arange(16, dtype=jnp.int32) == here).astype(WIDE)[:, None]
    first_half, second_half = (0, 1, 2, 4), (3, 5, 6, 7)
    pick = lambda blocks, half: [blocks[index] for index in half]
    results = []
    for half in (first_half, second_half):
        mine_here = after(mine, [result[5] for result in results])
        results.append(
            units_forward_back(
                pick(n_blocks, half), pick(g_blocks, half), small_rows, mine_here, unit_weights
            )
        )
    d_blocks = [None] * 8
    for half, result in zip((first_half, second_half), results):
        for place, index in enumerate(half):
            d_blocks[index] = result[place]
    (back_first, hidden_first), (back_second, hidden_second) = (
        results[0][4:],
        results[1][4:],
    )
    in_halves = lambda blocks: pick(blocks, first_half) + pick(blocks, second_half)
    weight_qkv_all = lax.all_gather(
        after(w_qkv.transpose(1, 0, 2), branch), "fsdp", axis=0, tiled=False
    )
    d_first = scatter_first(d_blocks)
    d_second = scatter_second(d_blocks, d_first)
    unit_part = outer_products(
        (back_first, back_second),
        (hidden_first, hidden_second),
        in_halves(n_blocks),
        in_halves(g_blocks),
    )
    unit_grads = lax.psum_scatter(unit_part, "fsdp", scatter_dimension=0, tiled=False)
    sums = scatter_sum(d_blocks[0], after(d_second, (unit_part, weight_qkv_all)))
    grad_sum = add_halves(sums[:, : width + 128])
    unit_first = large_first(unit_grads)

    logits = dot_rows(normed_own, gate_rows)
    probs_own = jax.nn.softmax(logits[:, :experts], axis=-1)
    gate_own = jax.nn.sigmoid(logits[:, experts : experts + 1])
    grad_normed, grad_combine = grad_sum[:, :width], grad_sum[:, width : width + experts]
    grad_gate = grad_sum[:, width + experts : width + experts + 1]
    picked = grad_combine * chosen
    grad_logits = low(
        probs_own * (picked - jnp.sum(picked * probs_own, axis=-1, keepdims=True))
    )
    grad_gate_logit = low(grad_gate * gate_own * (1.0 - gate_own))
    both = jnp.concatenate([grad_logits, grad_gate_logit], axis=1)
    grad_normed = grad_normed + dot_plain(both, gate_rows)
    grad_both = dot_columns(normed_own, both)
    grad_top = wide(grad_own)
    grad_gain_second = jnp.sum(grad_normed * middle * factor_second, axis=0)
    weighted = grad_normed * gain_second
    inner = jnp.mean(weighted * middle, axis=-1, keepdims=True)
    grad_middle = grad_top + weighted * factor_second - middle * factor_second**3 * inner
    grad_branch = low(grad_middle)

    grad_attended = branch_back(grad_branch, first_pack, heads * head_size)
    grad_heads = lax.all_to_all(
        grad_attended.reshape(rows, heads, head_size).transpose(1, 0, 2), "ctx", 0, 0, tiled=True
    ).reshape(rows * 8, head_size)
    grad_heads = after(grad_heads, unit_first)
    unit_second = large_second(unit_first)
    mixed = add_halves(after(sums[:, width + 128 :], grad_heads))
    result = low(valid * (middle + mixed))
    out_part = lax.psum_scatter(
        low(dot_columns(grad_branch, attended_own)), "fsdp", scatter_dimension=0, tiled=True
    )
    grad_proj, grad_bias = attend_back(queries, keys, values, grad_heads, cosine, sine)
    proj_own = lax.all_to_all(
        grad_proj.reshape(8, rows, 3 * head_size), "ctx", 0, 0, tiled=True
    )
    grad_qkv_here = low(dot_columns(normed_first, grad_proj))
    bias_rows = grad_bias.reshape(3, 8, bias_part).transpose(1, 0, 2).reshape(8, 3 * bias_part)
    bias_rows = jnp.pad(bias_rows, ((0, 0), (0, shard - 3 * bias_part))).reshape(width, 1)
    small_grads = low(jnp.concatenate([grad_both, grad_gain_second[:, None], bias_rows], axis=1))
    small_grads = jnp.pad(small_grads, ((0, 0), (0, 128 - small_grads.shape[1])))
    last_part = jnp.concatenate([grad_qkv_here, small_grads], axis=1)
    proj_own = after(proj_own, (last_part, unit_second))
    proj_own = proj_own.reshape(8, rows, 3, head_size).transpose(2, 1, 0, 3)
    proj_own = proj_own.reshape(3, rows, heads * head_size)
    first_part = first_back(proj_own, weight_qkv_all)
    grad_first = after(add_halves(first_part), result)
    unit_third = large_third(unit_second)
    factor_first = inverse_rms(hidden_in)
    weighted = grad_first * gain_first
    inner = jnp.mean(weighted * hidden_in, axis=-1, keepdims=True)
    grad_input = grad_middle + weighted * factor_first - hidden_in * factor_first**3 * inner

    last_pack = lax.psum_scatter(last_part, "fsdp", scatter_dimension=0, tiled=True)
    out_parts = out_part.reshape(shard, heads, head_size).transpose(1, 0, 2)
    out_parts = lax.all_to_all(after(out_parts, unit_second), "ctx", 0, 0, tiled=True)
    grad_w_o_here = low(jnp.sum(wide(out_parts), axis=0))
    unit_blocks = large_blocks(unit_grads, unit_first, unit_second, unit_third)
    early, late = (0, 1, 2, 4), (3, 5, 6, 7)
    placed = ()
    for half in (early, late):
        block_half = after(block_places, unit_second)[jnp.array(half)]
        placed = place_units(block_half, pick(unit_blocks, half), expert_units, placed)
    grad_egu, grad_edown, shared_grads = placed
    grad_w_sgu, grad_w_sdown = flip(shared_grads.reshape(3, 8 * shared_units, shard))
    weights_here = lax.dynamic_slice(
        w_qkv, (0, 0, here * head_size), (shard, 3, head_size)
    ).reshape(shard, 3 * head_size)
    products = jnp.sum(wide(weights_here) * wide(last_pack[:, : 3 * head_size]), axis=1)
    products = products + lax.ppermute(products, "tp", [(0, 1), (1, 0)])
    spare = 3 * head_size + experts + 3
    last_blocks = gather_relative(
        jnp.concatenate(
            [
                last_pack[:, :spare],
                low(products)[:, None],
                last_pack[:, spare + 1 :],
                grad_w_o_here,
            ],
            axis=1,
        )
    )
    grad_qkv, grad_w_o, small_sums = place_last(block_places, last_blocks)
    grad_w_qkv = grad_qkv.transpose(1, 0, 2)
    summed = jnp.sum(small_sums[:, :, : experts + 4], axis=0)
    grad_b_qkv = (
        small_sums[:, : 3 * bias_part, experts + 2].reshape(8, 3, bias_part).transpose(1, 0, 2)
    )
    grad_gain_first = summed[:, experts + 3] / wide(norm_gains[0])
    return (
        result,
        low(grad_input),
        jnp.stack([grad_gain_first, summed[:, experts + 1]]),
        grad_w_qkv,
        grad_b_qkv,
        grad_w_o,
        summed[:, :experts],
        summed[:, experts],
        grad_w_sgu,
        grad_w_sdown,
        grad_egu.transpose(3, 0, 1, 2),
        grad_edown.transpose(2, 0, 1),
    )


def solution(mesh):
    return jax.shard_map(
        body,
        mesh=mesh,
        in_specs=(
            P(("fsdp", "ctx"), None),
            P(),
            P(("fsdp", "ctx"), None),
            P(None, "fsdp"),
            P("fsdp", None, "tp"),
            P(None, "tp", "fsdp"),
            P("fsdp", "tp"),
            P("fsdp", None),
            P("fsdp"),
            P("fsdp", None, "tp"),
            P("fsdp", "tp"),
            P("fsdp", None, None, "tp"),
            P("fsdp", None, "tp"),
            P(("fsdp", "ctx"), None),
        ),
        out_specs=(
            P(("fsdp", "ctx"), None),
            P(("fsdp", "ctx"), None),
            P(None, "fsdp"),
            P("fsdp", None, "tp"),
            P(None, "tp", "fsdp"),
            P("fsdp", "tp"),
            P("fsdp", None),
            P("fsdp"),
            P("fsdp", None, "tp"),
            P("fsdp", "tp"),
            P("fsdp", None, None, "tp"),
            P("fsdp", None, "tp"),
        ),
        check_vma=False,
    )
```

```python
import jax
import jax.numpy as jnp
import numpy as np
from jax import lax
from jax.experimental import pallas as pl
from jax.experimental.pallas import tpu as pltpu
from jax.sharding import PartitionSpec as P

EPSILON = 1e-06
ROPE_BASE = 1000000.0
MASKED_SCORE = -1e30
LOW = jnp.bfloat16
WIDE = jnp.float32
VMEM_BYTES = 56 * 1024 * 1024


def low(values):
    return values.astype(LOW)


def wide(values):
    return values.astype(WIDE)


def rotary_tables(row_count, head_size):
    middle = head_size // 2
    powers = -(np.arange(middle, dtype=np.float32) * np.float32(2.0)) / np.float32(head_size)
    inverse = np.power(np.float32(ROPE_BASE), powers).astype(np.float32)
    places = np.arange(row_count, dtype=np.float32)
    angles = (places[:, None] * inverse[None, :]).astype(np.float32)
    cosine, sine = np.cos(angles), np.sin(angles)
    return (
        jnp.asarray(np.concatenate([cosine, cosine], axis=-1)),
        jnp.asarray(np.concatenate([-sine, sine], axis=-1)),
    )


def inverse_rms(values):
    return lax.rsqrt(jnp.mean(values * values, axis=-1, keepdims=True) + EPSILON)


def ring(step):
    return [(i, (i + step) % 8) for i in range(8)]


PAIR = [(i, i ^ 1) for i in range(8)]


def up(values):
    return lax.ppermute(values, "ctx", ring(2))


def down(values):
    return lax.ppermute(values, "ctx", ring(-2))


def swap(values):
    return lax.ppermute(values, "ctx", PAIR)


def relative_places():
    here = lax.axis_index("ctx")
    return [(here + step) % 8 for step in (0, 6, 2, 4)] + [
        ((here ^ 1) + step) % 8 for step in (0, 6, 2, 4)
    ]


def across(values):
    return lax.ppermute(values, "ctx", ring(4))


def gather_first(block):
    return up(block), down(block), swap(block), across(block)


def gather_second(first):
    _, _, pair, opposite = first
    return up(pair), down(pair), swap(opposite)


def gather_blocks(block, first, second):
    left, right, pair, opposite = first
    return [block, left, right, opposite, pair, *second]


def gather_relative(block):
    first = gather_first(block)
    return gather_blocks(block, first, gather_second(first))


def large_first(block):
    return up(block), down(block), swap(block)


def large_second(first):
    left, right, pair = first
    half = left.shape[0] // 2
    return up(left[:half]), down(right[half:]), up(pair), down(pair)


def large_third(second):
    _, _, pair_left, pair_right = second
    half = pair_left.shape[0] // 2
    return up(pair_left[:half]), down(pair_right[half:])


def large_blocks(block, first, second, third):
    left, right, pair = first
    opposite = jnp.concatenate(second[:2], axis=0)
    pair_opposite = jnp.concatenate(third, axis=0)
    return [block, left, right, opposite, pair, second[2], second[3], pair_opposite]


def scatter_first(blocks):
    _, _, _, _, _, pair_left, pair_right, pair_opposite = blocks
    return swap(low(pair_opposite)), up(low(pair_right)), down(low(pair_left))


def scatter_second(blocks, first):
    _, left, right, opposite, pair, _, _, _ = blocks
    from_pair, pair_up, pair_down = first
    return (
        across(low(wide(opposite) + wide(from_pair))),
        swap(low(wide(pair) + wide(pair_up) + wide(pair_down))),
        up(low(right)),
        down(low(left)),
    )


def scatter_sum(own, second):
    far, crossing, last_up, last_down = second
    return wide(own) + wide(far) + wide(crossing) + wide(last_up) + wide(last_down)


def scatter_relative(blocks):
    return scatter_sum(blocks[0], scatter_second(blocks, scatter_first(blocks)))


def add_halves(values):
    mine = low(values)
    return wide(mine) + wide(lax.ppermute(mine, "tp", [(0, 1), (1, 0)]))


QUERY_ROWS = 256


def estimate(flops, bytes_accessed):
    return pl.CostEstimate(
        flops=flops // 1000, bytes_accessed=bytes_accessed // 1000, transcendentals=0
    )


def params():
    return pltpu.CompilerParams(vmem_limit_bytes=VMEM_BYTES)


def turn(values, cosine, sine):
    return values * cosine + pltpu.roll(values, values.shape[-1] // 2, 1) * sine


def dot_plain(left, right):
    return jnp.dot(left, right, preferred_element_type=WIDE)


def dot_rows(left, right):
    return lax.dot_general(left, right, (((1,), (1,)), ((), ())), preferred_element_type=WIDE)


def dot_columns(left, right):
    return lax.dot_general(left, right, (((0,), (0,)), ((), ())), preferred_element_type=WIDE)


def probabilities(queries, keys, start, scale):
    scores = dot_rows(queries, keys) * scale
    rows = start + lax.broadcasted_iota(jnp.int32, scores.shape, 0)
    columns = lax.broadcasted_iota(jnp.int32, scores.shape, 1)
    scores = jnp.where(columns <= rows, scores, MASKED_SCORE)
    expons = jnp.exp(scores - jnp.max(scores, axis=-1, keepdims=True))
    return expons / jnp.sum(expons, axis=-1, keepdims=True)


def block_rows(place, rows):
    return pl.ds(pl.multiple_of(place * rows, rows), rows)


def attend_kernel(places_ref, *refs):
    blocks = refs[:8]
    weight_ref, gain_ref, bias_ref, cos_ref, sin_ref = refs[8:13]
    q_ref, k_ref, v_ref, out_ref, normed_ref = refs[13:]
    size = cos_ref.shape[1]
    scale = size ** (-0.5)
    gain = gain_ref[...]
    for index, block in enumerate(blocks):
        values = wide(block[...])
        normed = low(values * inverse_rms(values) * gain)
        normed_ref[block_rows(places_ref[index], block.shape[0]), :] = normed
    for start in range(0, q_ref.shape[0], QUERY_ROWS):
        end = start + QUERY_ROWS
        proj = dot_plain(normed_ref[start:end], weight_ref[:, : 3 * size]) + bias_ref[...]
        cosine, sine = cos_ref[start:end], sin_ref[start:end]
        q_ref[start:end] = low(turn(proj[:, :size], cosine, sine))
        k_ref[start:end] = low(turn(proj[:, size : 2 * size], cosine, sine))
        v_ref[start:end] = low(proj[:, 2 * size :])
    for start in range(0, q_ref.shape[0], QUERY_ROWS):
        end = start + QUERY_ROWS
        probs = low(probabilities(q_ref[start:end], k_ref[:end], start, scale))
        out_ref[start:end] = low(dot_plain(probs, v_ref[:end]))


def attend(places, blocks, pack, gain, bias, cosine, sine):
    rows, size = cosine.shape
    width = blocks[0].shape[1]
    one = jax.ShapeDtypeStruct((rows, size), LOW)
    whole = pl.BlockSpec(memory_space=pltpu.VMEM)
    part = pl.BlockSpec((width, 512), lambda step: (0, 2))
    whole_of = lambda shape: pl.BlockSpec(shape, lambda step: (0, 0))
    return pl.pallas_call(
        attend_kernel,
        grid=(1,),
        in_specs=[pl.BlockSpec(memory_space=pltpu.SMEM)]
        + [whole_of(block.shape) for block in blocks]
        + [part]
        + [whole_of(value.shape) for value in (gain, bias, cosine, sine)],
        out_specs=[whole_of((rows, size))] * 4 + [whole_of((rows, width))],
        out_shape=(one, one, one, one, jax.ShapeDtypeStruct((rows, width), LOW)),
        compiler_params=params(),
        cost_estimate=estimate(9_000_000_000, 12_000_000),
        name="attend",
    )(places, *blocks, pack, gain, bias, cosine, sine)


def attend_back_kernel(
    q_ref, k_ref, v_ref, grad_ref, cos_ref, sin_ref, out_ref, bias_ref, dk_ref, dv_ref
):
    size = cos_ref.shape[1]
    scale = size ** (-0.5)
    dk_ref[...] = jnp.zeros_like(dk_ref)
    dv_ref[...] = jnp.zeros_like(dv_ref)
    bias = jnp.zeros((1, size), WIDE)
    for start in range(0, q_ref.shape[0], QUERY_ROWS):
        end = start + QUERY_ROWS
        queries, grads = q_ref[start:end], grad_ref[start:end]
        probs = probabilities(queries, k_ref[:end], start, scale)
        grad_probs = dot_rows(grads, v_ref[:end])
        inner = jnp.sum(probs * grad_probs, axis=-1, keepdims=True)
        grad_scores = low(probs * (grad_probs - inner))
        grad_queries = dot_plain(grad_scores, k_ref[:end]) * scale
        grad_queries = low(turn(grad_queries, cos_ref[start:end], -sin_ref[start:end]))
        out_ref[start:end, :size] = grad_queries
        bias = bias + jnp.sum(wide(grad_queries), axis=0, keepdims=True)
        dk_ref[:end] += dot_columns(grad_scores, queries) * scale
        dv_ref[:end] += dot_columns(low(probs), grads)
    bias_ref[:, :size] = bias
    grad_keys = low(turn(dk_ref[...], cos_ref[...], -sin_ref[...]))
    out_ref[:, size : 2 * size] = grad_keys
    bias_ref[:, size : 2 * size] = jnp.sum(wide(grad_keys), axis=0, keepdims=True)
    grad_values = low(dv_ref[...])
    out_ref[:, 2 * size :] = grad_values
    bias_ref[:, 2 * size :] = jnp.sum(wide(grad_values), axis=0, keepdims=True)


def attend_back(queries, keys, values, grads, cosine, sine):
    rows, size = cosine.shape
    return pl.pallas_call(
        attend_back_kernel,
        out_shape=(
            jax.ShapeDtypeStruct((rows, 3 * size), LOW),
            jax.ShapeDtypeStruct((1, 3 * size), WIDE),
        ),
        scratch_shapes=[pltpu.VMEM((rows, size), WIDE), pltpu.VMEM((rows, size), WIDE)],
        compiler_params=params(),
        cost_estimate=estimate(7_000_000_000, 6_000_000),
        name="attend_back",
    )(queries, keys, values, grads, cosine, sine)


UNIT_ROWS = 16


def units_kernel(*refs):
    x_hbm, g_hbm = refs[:4], refs[4:8]
    small_ref, mine_ref, weight_hbm = refs[8:11]
    d_hbm, back_hbm, hidden_hbm = refs[11:15], refs[15], refs[16]
    weight_ref, x_ref, g_ref, tail_ref, gate_ref, up_ref, down_ref = refs[17:24]
    back_ref, hidden_ref, turned_ref, flat_ref, d_ref, sems = refs[24:]
    units, tokens = hidden_ref.shape
    rows, width = x_hbm[0].shape
    expert_units = units * 2 // 3
    count = 0
    started = {}

    def start(name, source, target):
        nonlocal count
        copy = pltpu.make_async_copy(source, target, sems.at[count])
        copy.start()
        count += 1
        started.setdefault(name, []).append(copy)

    def finish(name):
        for copy in started[name]:
            copy.wait()

    def start_weights(part):
        group = pl.ds(part * units, units)
        for index in range(8):
            columns = pl.ds(index * (width // 8), width // 8)
            start(part, weight_hbm.at[index, group, :], weight_ref.at[group, columns])

    block = lambda index: pl.ds(index * rows, rows)
    for index in range(4):
        start("x", x_hbm[index], x_ref.at[block(index)])
    start_weights(0)
    start_weights(1)
    for index in range(4):
        start("tail", g_hbm[index].at[:, pl.ds(width, 128)], tail_ref.at[block(index)])
        start("g", g_hbm[index].at[:, pl.ds(0, width)], g_ref.at[block(index)])
    start_weights(2)
    finish("x")
    logits = dot_rows(small_ref[...], x_ref[...])
    places = lax.broadcasted_iota(jnp.int32, logits.shape, 0)
    routed = jnp.where(places < 8, logits, MASKED_SCORE)
    expons = jnp.exp(routed - jnp.max(routed, axis=0, keepdims=True))
    probs = expons / jnp.sum(expons, axis=0, keepdims=True)
    shared_gate = jax.nn.sigmoid(
        jnp.sum(jnp.where(places == 8, logits, 0.0), axis=0, keepdims=True)
    )
    for part, (target, source) in enumerate(((gate_ref, x_ref), (up_ref, x_ref), (down_ref, g_ref))):
        if part == 2:
            finish("g")
        finish(part)
        target[...] = dot_rows(weight_ref[part * units : (part + 1) * units], source[...])
    finish("tail")
    chosen = wide(tail_ref[...]).T[: places.shape[0]]
    mine = mine_ref[...]
    combine = jnp.sum(probs * chosen * mine, axis=0, keepdims=True)

    def unit_rows(scale):
        def step(index, total):
            chunk = pl.ds(pl.multiple_of(index * UNIT_ROWS, UNIT_ROWS), UNIT_ROWS)
            after = pl.ds(pl.multiple_of(units + index * UNIT_ROWS, UNIT_ROWS), UNIT_ROWS)
            gate, upper, back = gate_ref[chunk, :], up_ref[chunk, :], down_ref[chunk, :]
            sigmoid = jax.nn.sigmoid(gate)
            silu = gate * sigmoid
            hidden = silu * upper
            hidden_ref[chunk, :] = low(hidden * scale)
            grad_hidden = back * scale
            back_ref[chunk, :] = low(grad_hidden * upper * (sigmoid + silu * (1.0 - sigmoid)))
            back_ref[after, :] = low(grad_hidden * silu)
            return total + hidden * back

        return step

    zeros = jnp.zeros((UNIT_ROWS, tokens), WIDE)
    middle, last = expert_units // UNIT_ROWS, units // UNIT_ROWS
    expert_sum = lax.fori_loop(0, middle, unit_rows(combine), zeros)
    shared_sum = lax.fori_loop(middle, last, unit_rows(shared_gate), zeros)
    start("out", hidden_ref, hidden_hbm)
    start("out", back_ref, back_hbm)
    expert_sum = jnp.sum(expert_sum, axis=0, keepdims=True)
    shared_sum = jnp.sum(shared_sum, axis=0, keepdims=True)
    sums = mine * expert_sum + jnp.where(places == 8, shared_sum, 0.0)
    sums = jnp.concatenate([sums, jnp.zeros((128 - sums.shape[0], tokens), WIDE)], axis=0)
    d_ref[:, width : width + 128] = low(sums.T)
    turned_ref[...] = back_ref[...].T
    step = width // 4

    def send(begin, size):
        for index in range(4):
            source = d_ref.at[block(index), pl.ds(begin, size)]
            start("out", source, d_hbm[index].at[:, pl.ds(begin, size)])

    for part in range(4):
        columns = slice(part * step, (part + 1) * step)
        d_ref[:, columns] = low(dot_plain(turned_ref[...], weight_ref[: 2 * units, columns]))
        send(part * step, step if part < 3 else step + 128)
    flat_ref[...] = hidden_ref[...].T
    for part in range(4):
        columns = slice(part * step, (part + 1) * step)
        begin = width + 128 + part * step
        d_ref[:, begin : begin + step] = low(
            dot_plain(flat_ref[...], weight_ref[2 * units :, columns])
        )
        send(begin, step)
    finish("out")


def units_forward_back(x_blocks, g_blocks, small_rows, mine, weights):
    rows, width = x_blocks[0].shape
    tokens = 4 * rows
    units = weights.shape[1] // 3
    vmem = pl.BlockSpec(memory_space=pltpu.VMEM)
    anywhere = pl.BlockSpec(memory_space=pl.ANY)
    return pl.pallas_call(
        units_kernel,
        in_specs=[anywhere] * 8 + [vmem] * 2 + [anywhere],
        out_specs=[anywhere] * 6,
        out_shape=[jax.ShapeDtypeStruct((rows, 2 * width + 128), LOW)] * 4
        + [
            jax.ShapeDtypeStruct((2 * units, tokens), LOW),
            jax.ShapeDtypeStruct((units, tokens), LOW),
        ],
        scratch_shapes=[
            pltpu.VMEM((3 * units, width), LOW),
            pltpu.VMEM((tokens, width), LOW),
            pltpu.VMEM((tokens, width), LOW),
            pltpu.VMEM((tokens, 128), LOW),
            pltpu.VMEM((units, tokens), WIDE),
            pltpu.VMEM((units, tokens), WIDE),
            pltpu.VMEM((units, tokens), WIDE),
            pltpu.VMEM((2 * units, tokens), LOW),
            pltpu.VMEM((units, tokens), LOW),
            pltpu.VMEM((tokens, 2 * units), LOW),
            pltpu.VMEM((tokens, units), LOW),
            pltpu.VMEM((tokens, 2 * width + 128), LOW),
            pltpu.SemaphoreType.DMA((70,)),
        ],
        compiler_params=params(),
        cost_estimate=estimate(11_000_000_000, 20_000_000),
        name="units",
    )(*x_blocks, *g_blocks, small_rows, mine, weights)


def outer_kernel(*refs):
    back_refs, hidden_refs, x_refs, g_refs, out_ref = (
        refs[:2],
        refs[2:4],
        refs[4:12],
        refs[12:20],
        refs[20],
    )
    units = hidden_refs[0].shape[0]

    def product(lefts, rights):
        halves = [
            jnp.concatenate([ref[...] for ref in rights[half : half + 4]], axis=0)
            for half in (0, 4)
        ]
        return low(dot_plain(lefts[0][...], halves[0]) + dot_plain(lefts[1][...], halves[1]))

    back, hidden = product(back_refs, x_refs), product(hidden_refs, g_refs)
    for index in range(out_ref.shape[0]):
        columns = slice(index * 256, (index + 1) * 256)
        out_ref[index, : 2 * units] = back[:, columns]
        out_ref[index, 2 * units :] = hidden[:, columns]


def outer_products(backs, hiddens, x_blocks, g_blocks):
    units, tokens = hiddens[0].shape
    rows = x_blocks[0].shape[0]
    whole = lambda value: pl.BlockSpec(value.shape, lambda step: (0, 0))
    return pl.pallas_call(
        outer_kernel,
        grid=(4,),
        in_specs=[whole(value) for value in (*backs, *hiddens)]
        + [pl.BlockSpec((rows, 512), lambda step: (0, step))] * 16,
        out_specs=pl.BlockSpec((2, 3 * units, 256), lambda step: (step, 0, 0)),
        out_shape=jax.ShapeDtypeStruct((8, 3 * units, 256), LOW),
        compiler_params=params(),
        cost_estimate=estimate(units * 2 * 1024 * 2048, 10_000_000),
        name="outer",
    )(*backs, *hiddens, *x_blocks, *g_blocks)


def pack_kernel(here_ref, qkv_ref, out_weight_ref, small_ref, out_ref):
    width, size = out_weight_ref.shape[1], qkv_ref.shape[2]
    out_ref[:, :width] = out_weight_ref[...]
    for index in range(3):
        out_ref[:, width + index * size : width + (index + 1) * size] = qkv_ref[index]
    out_ref[:, width + 3 * size :] = jnp.zeros_like(out_ref[:, width + 3 * size :])
    out_ref[: small_ref.shape[0], width + 3 * size :] = small_ref[...]


def pack_first(here, qkv, out_weight, small):
    shard, width = out_weight.shape
    return pl.pallas_call(
        pack_kernel,
        grid_spec=pltpu.PrefetchScalarGridSpec(
            num_scalar_prefetch=1,
            grid=(1,),
            in_specs=[
                pl.BlockSpec((3, shard, 128), lambda step, here_ref: (0, 0, here_ref[0])),
                pl.BlockSpec((shard, width), lambda step, here_ref: (0, 0)),
                pl.BlockSpec(small.shape, lambda step, here_ref: (0, 0)),
            ],
            out_specs=pl.BlockSpec((shard, width + 512), lambda step, here_ref: (0, 0)),
        ),
        out_shape=jax.ShapeDtypeStruct((shard, width + 512), LOW),
        cost_estimate=estimate(1000, 1000),
        name="pack",
    )(here, qkv, out_weight, small)


def branch_kernel(left_ref, weight_ref, out_ref):
    out_ref[...] = low(dot_rows(left_ref[...], weight_ref[...]))


def branch_part(attended, pack):
    rows, units = attended.shape
    width = pack.shape[0]
    return pl.pallas_call(
        branch_kernel,
        grid=(4,),
        in_specs=[
            pl.BlockSpec((rows, units), lambda step: (0, 0)),
            pl.BlockSpec((width // 4, units), lambda step: (step, 0)),
        ],
        out_specs=pl.BlockSpec((rows, width // 4), lambda step: (0, step)),
        out_shape=jax.ShapeDtypeStruct((rows, width), LOW),
        cost_estimate=estimate(600_000_000, 5_000_000),
        name="branch",
    )(attended, pack)


def branch_back_kernel(left_ref, weight_ref, out_ref):
    out_ref[...] = low(dot_plain(left_ref[...], weight_ref[...]))


def branch_back(grads, pack, units):
    rows, width = grads.shape
    return pl.pallas_call(
        branch_back_kernel,
        grid=(4,),
        in_specs=[
            pl.BlockSpec((rows, width), lambda step: (0, 0)),
            pl.BlockSpec((width, units // 4), lambda step: (0, step)),
        ],
        out_specs=pl.BlockSpec((rows, units // 4), lambda step: (0, step)),
        out_shape=jax.ShapeDtypeStruct((rows, units), LOW),
        cost_estimate=estimate(600_000_000, 5_000_000),
        name="branch_back",
    )(grads, pack)


def first_back_kernel(left_ref, weight_ref, out_ref):
    total = dot_rows(left_ref[0], weight_ref[0, 0])
    for part in (1, 2):
        total = total + dot_rows(left_ref[part], weight_ref[0, part])
    out_ref[...] = low(total)


def first_back(grads, weights):
    parts, rows, units = grads.shape
    shards, _, shard, _ = weights.shape
    return pl.pallas_call(
        first_back_kernel,
        grid=(shards,),
        in_specs=[
            pl.BlockSpec((parts, rows, units), lambda step: (0, 0, 0)),
            pl.BlockSpec((1, parts, shard, units), lambda step: (step, 0, 0, 0)),
        ],
        out_specs=pl.BlockSpec((rows, shard), lambda step: (0, step)),
        out_shape=jax.ShapeDtypeStruct((rows, shards * shard), LOW),
        cost_estimate=estimate(1_700_000_000, 13_000_000),
        name="first_back",
    )(grads, weights)


def place_kernel(places_ref, *refs):
    blocks = refs[:8]
    qkv_ref, out_ref, small_ref = refs[8:]
    for index, block in enumerate(blocks):
        columns = block_rows(places_ref[index], 128)
        for part in range(3):
            qkv_ref[part, :, columns] = wide(block[:, part * 128 : (part + 1) * 128])
        out_ref[:, columns] = wide(block[:, 512:640])
        small_ref[places_ref[index]] = wide(block[:, 384:512])


def place_last(places, blocks):
    shard = blocks[0].shape[0]
    vmem = pl.BlockSpec(memory_space=pltpu.VMEM)
    return pl.pallas_call(
        place_kernel,
        in_specs=[pl.BlockSpec(memory_space=pltpu.SMEM)] + [vmem] * 8,
        out_specs=[vmem] * 3,
        out_shape=(
            jax.ShapeDtypeStruct((3, shard, 1024), WIDE),
            jax.ShapeDtypeStruct((shard, 1024), WIDE),
            jax.ShapeDtypeStruct((8, shard, 128), WIDE),
        ),
        compiler_params=params(),
        cost_estimate=estimate(1000, 1000),
        name="place",
    )(places, *blocks)


def place_units_kernel(places_ref, *refs):
    blocks, (gate_ref, down_ref, shared_ref) = refs[:4], refs[-3:]
    expert_units = down_ref.shape[1]
    units = blocks[0].shape[0] // 3
    step = pl.program_id(0)
    for index, block in enumerate(blocks):

        @pl.when(step == index)
        def _(block=block):
            for part in range(3):
                start = part * units
                expert = wide(block[start : start + expert_units])
                if part < 2:
                    gate_ref[0, part] = expert
                else:
                    down_ref[0] = expert
                shared_ref[part, 0] = block[start + expert_units : start + units]


def place_units(places, blocks, expert_units, earlier):
    total, shard = blocks[0].shape
    shared_units = total // 3 - expert_units
    outs = (
        jax.ShapeDtypeStruct((8, 2, expert_units, shard), WIDE),
        jax.ShapeDtypeStruct((8, expert_units, shard), WIDE),
        jax.ShapeDtypeStruct((3, 8, shared_units, shard), LOW),
    )
    anywhere = pl.BlockSpec(memory_space=pl.ANY)
    return pl.pallas_call(
        place_units_kernel,
        grid_spec=pltpu.PrefetchScalarGridSpec(
            num_scalar_prefetch=1,
            grid=(4,),
            in_specs=[pl.BlockSpec((total, shard), lambda step, places_ref: (0, 0))] * 4
            + [anywhere] * len(earlier),
            out_specs=[
                pl.BlockSpec(
                    (1, 2, expert_units, shard),
                    lambda step, places_ref: (places_ref[step], 0, 0, 0),
                ),
                pl.BlockSpec(
                    (1, expert_units, shard),
                    lambda step, places_ref: (places_ref[step], 0, 0),
                ),
                pl.BlockSpec(
                    (3, 1, shared_units, shard),
                    lambda step, places_ref: (0, places_ref[step], 0, 0),
                ),
            ],
        ),
        out_shape=outs,
        input_output_aliases={5 + index: index for index in range(len(earlier))},
        compiler_params=params(),
        cost_estimate=estimate(1000, 1000),
        name="place_units",
    )(places, *blocks, *earlier)


def flip_kernel(one_ref, in_ref, gate_ref, down_ref):
    for part in range(2):
        gate_ref[:, part, :] = dot_rows(one_ref[...], in_ref[part])
    down_ref[...] = dot_rows(one_ref[...], in_ref[2])


def flip(values):
    parts, units, shard = values.shape
    return pl.pallas_call(
        flip_kernel,
        grid=(2,),
        in_specs=[
            pl.BlockSpec((shard, shard), lambda step: (0, 0)),
            pl.BlockSpec((parts, units // 2, shard), lambda step: (0, step, 0)),
        ],
        out_specs=[
            pl.BlockSpec((shard, 2, units // 2), lambda step: (0, 0, step)),
            pl.BlockSpec((shard, units // 2), lambda step: (0, step)),
        ],
        out_shape=(
            jax.ShapeDtypeStruct((shard, 2, units), WIDE),
            jax.ShapeDtypeStruct((shard, units), WIDE),
        ),
        compiler_params=params(),
        cost_estimate=estimate(1000, 1000),
        name="flip",
    )(jnp.eye(shard, dtype=LOW), values)


def after(values, earlier):
    return lax.optimization_barrier((values, earlier))[0]


def body(
    inputs,
    lengths,
    routes,
    norm_gains,
    w_qkv,
    b_qkv,
    w_o,
    w_router,
    w_sgate,
    w_sgu,
    w_sdown,
    w_egu,
    w_edown,
    grad_out,
):
    rows, width = inputs.shape
    shard = w_qkv.shape[0]
    experts = w_egu.shape[1]
    heads, bias_part = b_qkv.shape[1], b_qkv.shape[2]
    head_size = bias_part * 8
    expert_units = w_edown.shape[2]
    shared_units = w_sdown.shape[1] // 8
    units = expert_units + shared_units
    group, here = lax.axis_index("fsdp"), lax.axis_index("ctx")
    places = here * rows + jnp.arange(rows, dtype=jnp.int32)
    length_here = lax.dynamic_index_in_dim(lengths, group, 0, keepdims=False)
    valid = (places < length_here).astype(WIDE)[:, None]
    experts_range = jnp.arange(experts, dtype=jnp.int32)
    chosen = (
        jnp.any(routes[:, :, None] == experts_range[None, None, :], axis=1).astype(WIDE) * valid
    )
    block_places = jnp.stack(relative_places()).astype(jnp.int32)

    bias_here = lax.dynamic_slice(b_qkv, (0, here, 0), (3, 1, bias_part)).reshape(1, 3 * bias_part)
    small = jnp.concatenate(
        [
            w_router.T,
            w_sgate[None],
            norm_gains,
            jnp.pad(bias_here, ((0, 0), (0, shard - 3 * bias_part))),
            jnp.zeros((4, shard), LOW),
        ],
        axis=0,
    )
    first_pack = lax.all_gather(
        pack_first(
            here.astype(jnp.int32).reshape(1),
            w_qkv.transpose(1, 0, 2),
            w_o,
            small.reshape(32, 128),
        ),
        "fsdp",
        axis=0,
        tiled=True,
    )
    small_all = first_pack[:, 1408:].reshape(8, shard, 128)[:, :32].reshape(8, 16, shard)
    small_all = small_all.transpose(1, 0, 2)
    bias_all = small_all[11, :, : 3 * bias_part].reshape(8, 3, bias_part)
    bias_all = wide(bias_all.transpose(1, 0, 2).reshape(1, 3 * head_size))
    small_all = small_all.reshape(16, width)
    gain_first, gain_second = wide(small_all[9]), wide(small_all[10])
    gate_rows = small_all[: experts + 1]
    small_rows = jnp.pad(gate_rows, ((0, 16 - experts - 1), (0, 0)))
    x_first = gather_first(inputs)
    x_second = gather_second(x_first)
    grad_own = low(wide(grad_out) * valid)
    grad_pack = jnp.concatenate(
        [grad_own, jnp.pad(low(chosen), ((0, 0), (0, 128 - experts)))], axis=1
    )
    here_late = after(here, (x_first, x_second, grad_pack, block_places))
    shared_start = here_late * shared_units
    shared_gu = lax.dynamic_slice(w_sgu, (0, 0, shared_start), (shard, 2, shared_units))
    shared_gu = shared_gu.transpose(1, 2, 0)
    shared_down = lax.dynamic_slice(w_sdown, (0, shared_start), (shard, shared_units)).T
    expert_gu = lax.dynamic_index_in_dim(w_egu.transpose(1, 2, 3, 0), here_late, 0, keepdims=False)
    expert_down = lax.dynamic_index_in_dim(w_edown.transpose(1, 2, 0), here_late, 0, keepdims=False)
    unit_weights = lax.all_gather(
        jnp.concatenate(
            [expert_gu[0], shared_gu[0], expert_gu[1], shared_gu[1], expert_down, shared_down],
            axis=0,
        ),
        "fsdp",
        axis=0,
        tiled=False,
    )

    cosine, sine = rotary_tables(rows * 8, head_size)
    hidden_in = wide(inputs)
    x_blocks = gather_blocks(inputs, x_first, x_second)
    grad_pack = after(grad_pack, x_second)
    g_first = gather_first(grad_pack)
    g_second = gather_second(g_first)
    g_blocks = gather_blocks(grad_pack, g_first, g_second)
    queries, keys, values, attended, normed_first = attend(
        block_places, x_blocks, first_pack, gain_first[None], bias_all, cosine, sine
    )
    attended_own = lax.all_to_all(attended, "ctx", 0, 1, tiled=True)
    branch = add_halves(after(branch_part(attended_own, first_pack), g_first))
    middle = hidden_in + branch
    factor_second = inverse_rms(middle)
    normed_own = low(middle * factor_second * gain_second)

    n_first = gather_first(normed_own)
    n_second = gather_second(n_first)
    n_blocks = gather_blocks(normed_own, n_first, n_second)
    mine = (jnp.arange(16, dtype=jnp.int32) == here).astype(WIDE)[:, None]
    first_half, second_half = (0, 1, 2, 4), (3, 5, 6, 7)
    pick = lambda blocks, half: [blocks[index] for index in half]
    results = []
    for half in (first_half, second_half):
        mine_here = after(mine, [result[5] for result in results])
        results.append(
            units_forward_back(
                pick(n_blocks, half), pick(g_blocks, half), small_rows, mine_here, unit_weights
            )
        )
    d_blocks = [None] * 8
    for half, result in zip((first_half, second_half), results):
        for place, index in enumerate(half):
            d_blocks[index] = result[place]
    (back_first, hidden_first), (back_second, hidden_second) = (
        results[0][4:],
        results[1][4:],
    )
    in_halves = lambda blocks: pick(blocks, first_half) + pick(blocks, second_half)
    weight_qkv_all = lax.all_gather(
        after(w_qkv.transpose(1, 0, 2), branch), "fsdp", axis=0, tiled=False
    )
    d_first = scatter_first(d_blocks)
    d_second = scatter_second(d_blocks, d_first)
    unit_part = outer_products(
        (back_first, back_second),
        (hidden_first, hidden_second),
        in_halves(n_blocks),
        in_halves(g_blocks),
    )
    unit_grads = lax.psum_scatter(unit_part, "fsdp", scatter_dimension=0, tiled=False)
    sums = scatter_sum(d_blocks[0], after(d_second, (unit_part, weight_qkv_all)))
    grad_sum = add_halves(sums[:, : width + 128])
    unit_first = large_first(unit_grads)

    logits = dot_rows(normed_own, gate_rows)
    probs_own = jax.nn.softmax(logits[:, :experts], axis=-1)
    gate_own = jax.nn.sigmoid(logits[:, experts : experts + 1])
    grad_normed, grad_combine = grad_sum[:, :width], grad_sum[:, width : width + experts]
    grad_gate = grad_sum[:, width + experts : width + experts + 1]
    picked = grad_combine * chosen
    grad_logits = low(
        probs_own * (picked - jnp.sum(picked * probs_own, axis=-1, keepdims=True))
    )
    grad_gate_logit = low(grad_gate * gate_own * (1.0 - gate_own))
    both = jnp.concatenate([grad_logits, grad_gate_logit], axis=1)
    grad_normed = grad_normed + dot_plain(both, gate_rows)
    grad_both = dot_columns(normed_own, both)
    grad_top = wide(grad_own)
    grad_gain_second = jnp.sum(grad_normed * middle * factor_second, axis=0)
    weighted = grad_normed * gain_second
    inner = jnp.mean(weighted * middle, axis=-1, keepdims=True)
    grad_middle = grad_top + weighted * factor_second - middle * factor_second**3 * inner
    grad_branch = low(grad_middle)

    grad_attended = branch_back(grad_branch, first_pack, heads * head_size)
    grad_heads = lax.all_to_all(
        grad_attended.reshape(rows, heads, head_size).transpose(1, 0, 2), "ctx", 0, 0, tiled=True
    ).reshape(rows * 8, head_size)
    grad_heads = after(grad_heads, unit_first)
    unit_second = large_second(unit_first)
    mixed = add_halves(after(sums[:, width + 128 :], grad_heads))
    result = low(valid * (middle + mixed))
    out_part = lax.psum_scatter(
        low(dot_columns(grad_branch, attended_own)), "fsdp", scatter_dimension=0, tiled=True
    )
    grad_proj, grad_bias = attend_back(queries, keys, values, grad_heads, cosine, sine)
    out_parts = out_part.reshape(shard, heads, head_size).transpose(1, 0, 2)
    out_parts = lax.all_to_all(after(out_parts, grad_proj), "ctx", 0, 0, tiled=True)
    grad_w_o_here = low(jnp.sum(wide(out_parts), axis=0))
    proj_own = lax.all_to_all(
        grad_proj.reshape(8, rows, 3 * head_size), "ctx", 0, 0, tiled=True
    )
    grad_qkv_here = low(dot_columns(normed_first, grad_proj))
    bias_rows = grad_bias.reshape(3, 8, bias_part).transpose(1, 0, 2).reshape(8, 3 * bias_part)
    bias_rows = jnp.pad(bias_rows, ((0, 0), (0, shard - 3 * bias_part))).reshape(width, 1)
    small_grads = low(jnp.concatenate([grad_both, grad_gain_second[:, None], bias_rows], axis=1))
    small_grads = jnp.pad(small_grads, ((0, 0), (0, 128 - small_grads.shape[1])))
    last_part = jnp.concatenate([grad_qkv_here, small_grads], axis=1)
    proj_own = after(proj_own, (last_part, unit_second, grad_w_o_here))
    proj_own = proj_own.reshape(8, rows, 3, head_size).transpose(2, 1, 0, 3)
    proj_own = proj_own.reshape(3, rows, heads * head_size)
    first_part = first_back(proj_own, weight_qkv_all)
    last_pack = lax.psum_scatter(last_part, "fsdp", scatter_dimension=0, tiled=True)
    weights_here = lax.dynamic_slice(
        w_qkv, (0, 0, here * head_size), (shard, 3, head_size)
    ).reshape(shard, 3 * head_size)
    products = jnp.sum(wide(weights_here) * wide(last_pack[:, : 3 * head_size]), axis=1)
    products = products + lax.ppermute(products, "tp", [(0, 1), (1, 0)])
    spare = 3 * head_size + experts + 3
    last_block = (
        jnp.concatenate(
            [
                last_pack[:, :spare],
                low(products)[:, None],
                last_pack[:, spare + 1 :],
                grad_w_o_here,
            ],
            axis=1,
        )
    )
    last_first = gather_first(last_block)
    unit_third = large_third(unit_second)
    grad_first = after(add_halves(after(first_part, last_first)), (result, unit_third))
    last_blocks = gather_blocks(last_block, last_first, gather_second(last_first))
    factor_first = inverse_rms(hidden_in)
    weighted = grad_first * gain_first
    inner = jnp.mean(weighted * hidden_in, axis=-1, keepdims=True)
    grad_input = grad_middle + weighted * factor_first - hidden_in * factor_first**3 * inner

    unit_blocks = large_blocks(unit_grads, unit_first, unit_second, unit_third)
    early, late = (0, 1, 2, 4), (3, 5, 6, 7)
    placed = ()
    for half in (early, late):
        block_half = after(block_places, unit_second)[jnp.array(half)]
        placed = place_units(block_half, pick(unit_blocks, half), expert_units, placed)
    grad_egu, grad_edown, shared_grads = placed
    grad_w_sgu, grad_w_sdown = flip(shared_grads.reshape(3, 8 * shared_units, shard))
    grad_qkv, grad_w_o, small_sums = place_last(block_places, last_blocks)
    grad_w_qkv = grad_qkv.transpose(1, 0, 2)
    summed = jnp.sum(small_sums[:, :, : experts + 4], axis=0)
    grad_b_qkv = (
        small_sums[:, : 3 * bias_part, experts + 2].reshape(8, 3, bias_part).transpose(1, 0, 2)
    )
    grad_gain_first = summed[:, experts + 3] / wide(norm_gains[0])
    return (
        result,
        low(grad_input),
        jnp.stack([grad_gain_first, summed[:, experts + 1]]),
        grad_w_qkv,
        grad_b_qkv,
        grad_w_o,
        summed[:, :experts],
        summed[:, experts],
        grad_w_sgu,
        grad_w_sdown,
        grad_egu.transpose(3, 0, 1, 2),
        grad_edown.transpose(2, 0, 1),
    )


def solution(mesh):
    return jax.shard_map(
        body,
        mesh=mesh,
        in_specs=(
            P(("fsdp", "ctx"), None),
            P(),
            P(("fsdp", "ctx"), None),
            P(None, "fsdp"),
            P("fsdp", None, "tp"),
            P(None, "tp", "fsdp"),
            P("fsdp", "tp"),
            P("fsdp", None),
            P("fsdp"),
            P("fsdp", None, "tp"),
            P("fsdp", "tp"),
            P("fsdp", None, None, "tp"),
            P("fsdp", None, "tp"),
            P(("fsdp", "ctx"), None),
        ),
        out_specs=(
            P(("fsdp", "ctx"), None),
            P(("fsdp", "ctx"), None),
            P(None, "fsdp"),
            P("fsdp", None, "tp"),
            P(None, "tp", "fsdp"),
            P("fsdp", "tp"),
            P("fsdp", None),
            P("fsdp"),
            P("fsdp", None, "tp"),
            P("fsdp", "tp"),
            P("fsdp", None, None, "tp"),
            P("fsdp", None, "tp"),
        ),
        check_vma=False,
    )
```

```python
import functools

import jax
import jax.numpy as jnp
import numpy as np
from jax import lax
from jax.experimental import pallas as pl
from jax.experimental.pallas import tpu as pltpu
from jax.sharding import PartitionSpec as P

EPSILON = 1e-06
ROPE_BASE = 1000000.0
MASKED_SCORE = -1e30
LOW = jnp.bfloat16
WIDE = jnp.float32
VMEM_BYTES = 56 * 1024 * 1024


def low(values):
    return values.astype(LOW)


def wide(values):
    return values.astype(WIDE)


def rotary_tables(row_count, head_size):
    middle = head_size // 2
    powers = -(np.arange(middle, dtype=np.float32) * np.float32(2.0)) / np.float32(head_size)
    inverse = np.power(np.float32(ROPE_BASE), powers).astype(np.float32)
    places = np.arange(row_count, dtype=np.float32)
    angles = (places[:, None] * inverse[None, :]).astype(np.float32)
    cosine, sine = np.cos(angles), np.sin(angles)
    return (
        jnp.asarray(np.concatenate([cosine, cosine], axis=-1)),
        jnp.asarray(np.concatenate([-sine, sine], axis=-1)),
    )


def inverse_rms(values):
    return lax.rsqrt(jnp.mean(values * values, axis=-1, keepdims=True) + EPSILON)


def ring(step):
    return [(i, (i + step) % 8) for i in range(8)]


PAIR = [(i, i ^ 1) for i in range(8)]


def up(values):
    return lax.ppermute(values, "ctx", ring(2))


def down(values):
    return lax.ppermute(values, "ctx", ring(-2))


def swap(values):
    return lax.ppermute(values, "ctx", PAIR)


def relative_places():
    here = lax.axis_index("ctx")
    return [(here + step) % 8 for step in (0, 6, 2, 4)] + [
        ((here ^ 1) + step) % 8 for step in (0, 6, 2, 4)
    ]


def across(values):
    return lax.ppermute(values, "ctx", ring(4))


def gather_first(block):
    return up(block), down(block), swap(block), across(block)


def gather_second(first):
    _, _, pair, opposite = first
    return up(pair), down(pair), swap(opposite)


def gather_blocks(block, first, second):
    left, right, pair, opposite = first
    return [block, left, right, opposite, pair, *second]


def gather_relative(block):
    first = gather_first(block)
    return gather_blocks(block, first, gather_second(first))


def large_first(block):
    return up(block), down(block), swap(block)


def large_second(first):
    left, right, pair = first
    half = left.shape[0] // 2
    return up(left[:half]), down(right[half:]), up(pair), down(pair)


def large_third(second):
    _, _, pair_left, pair_right = second
    half = pair_left.shape[0] // 2
    return up(pair_left[:half]), down(pair_right[half:])


def large_blocks(block, first, second, third):
    left, right, pair = first
    opposite = jnp.concatenate(second[:2], axis=0)
    pair_opposite = jnp.concatenate(third, axis=0)
    return [block, left, right, opposite, pair, second[2], second[3], pair_opposite]


def scatter_first(blocks):
    _, _, _, _, _, pair_left, pair_right, pair_opposite = blocks
    return swap(low(pair_opposite)), up(low(pair_right)), down(low(pair_left))


def scatter_second(blocks, first):
    _, left, right, opposite, pair, _, _, _ = blocks
    from_pair, pair_up, pair_down = first
    return (
        across(low(wide(opposite) + wide(from_pair))),
        swap(low(wide(pair) + wide(pair_up) + wide(pair_down))),
        up(low(right)),
        down(low(left)),
    )


def scatter_sum(own, second):
    far, crossing, last_up, last_down = second
    return wide(own) + wide(far) + wide(crossing) + wide(last_up) + wide(last_down)


def scatter_relative(blocks):
    return scatter_sum(blocks[0], scatter_second(blocks, scatter_first(blocks)))


def add_halves(values):
    mine = low(values)
    return wide(mine) + wide(lax.ppermute(mine, "tp", [(0, 1), (1, 0)]))


QUERY_ROWS = 256


def estimate(flops, bytes_accessed):
    return pl.CostEstimate(
        flops=flops // 1000, bytes_accessed=bytes_accessed // 1000, transcendentals=0
    )


def params():
    return pltpu.CompilerParams(vmem_limit_bytes=VMEM_BYTES)


def turn(values, cosine, sine):
    return values * cosine + pltpu.roll(values, values.shape[-1] // 2, 1) * sine


def dot_plain(left, right):
    return jnp.dot(left, right, preferred_element_type=WIDE)


def dot_rows(left, right):
    return lax.dot_general(left, right, (((1,), (1,)), ((), ())), preferred_element_type=WIDE)


def dot_columns(left, right):
    return lax.dot_general(left, right, (((0,), (0,)), ((), ())), preferred_element_type=WIDE)


def probabilities(queries, keys, start, scale):
    scores = dot_rows(queries, keys) * scale
    rows = start + lax.broadcasted_iota(jnp.int32, scores.shape, 0)
    columns = lax.broadcasted_iota(jnp.int32, scores.shape, 1)
    scores = jnp.where(columns <= rows, scores, MASKED_SCORE)
    expons = jnp.exp(scores - jnp.max(scores, axis=-1, keepdims=True))
    return expons / jnp.sum(expons, axis=-1, keepdims=True)


def block_rows(place, rows):
    return pl.ds(pl.multiple_of(place * rows, rows), rows)


def attend_kernel(places_ref, *refs):
    blocks = refs[:8]
    weight_ref, gain_ref, bias_ref, cos_ref, sin_ref = refs[8:13]
    q_ref, k_ref, v_ref, out_ref, normed_ref = refs[13:]
    size = cos_ref.shape[1]
    scale = size ** (-0.5)
    gain = gain_ref[...]
    for index, block in enumerate(blocks):
        values = wide(block[...])
        normed = low(values * inverse_rms(values) * gain)
        normed_ref[block_rows(places_ref[index], block.shape[0]), :] = normed
    for start in range(0, q_ref.shape[0], QUERY_ROWS):
        end = start + QUERY_ROWS
        proj = dot_plain(normed_ref[start:end], weight_ref[:, : 3 * size]) + bias_ref[...]
        cosine, sine = cos_ref[start:end], sin_ref[start:end]
        q_ref[start:end] = low(turn(proj[:, :size], cosine, sine))
        k_ref[start:end] = low(turn(proj[:, size : 2 * size], cosine, sine))
        v_ref[start:end] = low(proj[:, 2 * size :])
    for start in range(0, q_ref.shape[0], QUERY_ROWS):
        end = start + QUERY_ROWS
        probs = low(probabilities(q_ref[start:end], k_ref[:end], start, scale))
        out_ref[start:end] = low(dot_plain(probs, v_ref[:end]))


def attend(places, blocks, pack, gain, bias, cosine, sine):
    rows, size = cosine.shape
    width = blocks[0].shape[1]
    one = jax.ShapeDtypeStruct((rows, size), LOW)
    whole = pl.BlockSpec(memory_space=pltpu.VMEM)
    part = pl.BlockSpec((width, 512), lambda step: (0, 2))
    whole_of = lambda shape: pl.BlockSpec(shape, lambda step: (0, 0))
    return pl.pallas_call(
        attend_kernel,
        grid=(1,),
        in_specs=[pl.BlockSpec(memory_space=pltpu.SMEM)]
        + [whole_of(block.shape) for block in blocks]
        + [part]
        + [whole_of(value.shape) for value in (gain, bias, cosine, sine)],
        out_specs=[whole_of((rows, size))] * 4 + [whole_of((rows, width))],
        out_shape=(one, one, one, one, jax.ShapeDtypeStruct((rows, width), LOW)),
        compiler_params=params(),
        cost_estimate=estimate(9_000_000_000, 12_000_000),
        name="attend",
    )(places, *blocks, pack, gain, bias, cosine, sine)


def attend_back_kernel(
    q_ref, k_ref, v_ref, grad_ref, cos_ref, sin_ref, out_ref, bias_ref, dk_ref, dv_ref
):
    size = cos_ref.shape[1]
    scale = size ** (-0.5)
    dk_ref[...] = jnp.zeros_like(dk_ref)
    dv_ref[...] = jnp.zeros_like(dv_ref)
    bias = jnp.zeros((1, size), WIDE)
    for start in range(0, q_ref.shape[0], QUERY_ROWS):
        end = start + QUERY_ROWS
        queries, grads = q_ref[start:end], grad_ref[start:end]
        probs = probabilities(queries, k_ref[:end], start, scale)
        grad_probs = dot_rows(grads, v_ref[:end])
        inner = jnp.sum(probs * grad_probs, axis=-1, keepdims=True)
        grad_scores = low(probs * (grad_probs - inner))
        grad_queries = dot_plain(grad_scores, k_ref[:end]) * scale
        grad_queries = low(turn(grad_queries, cos_ref[start:end], -sin_ref[start:end]))
        out_ref[start:end, :size] = grad_queries
        bias = bias + jnp.sum(wide(grad_queries), axis=0, keepdims=True)
        dk_ref[:end] += dot_columns(grad_scores, queries) * scale
        dv_ref[:end] += dot_columns(low(probs), grads)
    bias_ref[:, :size] = bias
    grad_keys = low(turn(dk_ref[...], cos_ref[...], -sin_ref[...]))
    out_ref[:, size : 2 * size] = grad_keys
    bias_ref[:, size : 2 * size] = jnp.sum(wide(grad_keys), axis=0, keepdims=True)
    grad_values = low(dv_ref[...])
    out_ref[:, 2 * size :] = grad_values
    bias_ref[:, 2 * size :] = jnp.sum(wide(grad_values), axis=0, keepdims=True)


def attend_back(queries, keys, values, grads, cosine, sine):
    rows, size = cosine.shape
    return pl.pallas_call(
        attend_back_kernel,
        out_shape=(
            jax.ShapeDtypeStruct((rows, 3 * size), LOW),
            jax.ShapeDtypeStruct((1, 3 * size), WIDE),
        ),
        scratch_shapes=[pltpu.VMEM((rows, size), WIDE), pltpu.VMEM((rows, size), WIDE)],
        compiler_params=params(),
        cost_estimate=estimate(7_000_000_000, 6_000_000),
        name="attend_back",
    )(queries, keys, values, grads, cosine, sine)


UNIT_ROWS = 16


def units_kernel(half, *refs):
    x_hbm, g_hbm = refs[:4], refs[4:8]
    small_ref, mine_ref, weight_hbm = refs[8:11]
    refs = refs[:11] + refs[11 + 2 * half :]
    d_hbm, back_hbm, hidden_hbm = refs[11:15], refs[15], refs[16]
    weight_ref, x_ref, g_ref, tail_ref, gate_ref, up_ref, down_ref = refs[17:24]
    back_ref, hidden_ref, turned_ref, flat_ref, d_ref, sems = refs[24:]
    units, tokens = hidden_ref.shape
    rows, width = x_hbm[0].shape
    expert_units = units * 2 // 3
    count = 0
    started = {}

    def start(name, source, target):
        nonlocal count
        copy = pltpu.make_async_copy(source, target, sems.at[count])
        copy.start()
        count += 1
        started.setdefault(name, []).append(copy)

    def finish(name):
        for copy in started[name]:
            copy.wait()

    def start_weights(part):
        group = pl.ds(part * units, units)
        for index in range(8):
            columns = pl.ds(index * (width // 8), width // 8)
            start(part, weight_hbm.at[index, group, :], weight_ref.at[group, columns])

    block = lambda index: pl.ds(index * rows, rows)
    for index in range(4):
        start("x", x_hbm[index], x_ref.at[block(index)])
    start_weights(0)
    start_weights(1)
    for index in range(4):
        start("tail", g_hbm[index].at[:, pl.ds(width, 128)], tail_ref.at[block(index)])
        start("g", g_hbm[index].at[:, pl.ds(0, width)], g_ref.at[block(index)])
    start_weights(2)
    finish("x")
    logits = dot_rows(small_ref[...], x_ref[...])
    places = lax.broadcasted_iota(jnp.int32, logits.shape, 0)
    routed = jnp.where(places < 8, logits, MASKED_SCORE)
    expons = jnp.exp(routed - jnp.max(routed, axis=0, keepdims=True))
    probs = expons / jnp.sum(expons, axis=0, keepdims=True)
    shared_gate = jax.nn.sigmoid(
        jnp.sum(jnp.where(places == 8, logits, 0.0), axis=0, keepdims=True)
    )
    for part, (target, source) in enumerate(((gate_ref, x_ref), (up_ref, x_ref), (down_ref, g_ref))):
        if part == 2:
            finish("g")
        finish(part)
        target[...] = dot_rows(weight_ref[part * units : (part + 1) * units], source[...])
    finish("tail")
    chosen = wide(tail_ref[...]).T[: places.shape[0]]
    mine = mine_ref[...]
    combine = jnp.sum(probs * chosen * mine, axis=0, keepdims=True)

    def unit_rows(scale):
        def step(index, total):
            chunk = pl.ds(pl.multiple_of(index * UNIT_ROWS, UNIT_ROWS), UNIT_ROWS)
            after = pl.ds(pl.multiple_of(units + index * UNIT_ROWS, UNIT_ROWS), UNIT_ROWS)
            gate, upper, back = gate_ref[chunk, :], up_ref[chunk, :], down_ref[chunk, :]
            sigmoid = jax.nn.sigmoid(gate)
            silu = gate * sigmoid
            hidden = silu * upper
            hidden_ref[chunk, :] = low(hidden * scale)
            grad_hidden = back * scale
            back_ref[chunk, :] = low(grad_hidden * upper * (sigmoid + silu * (1.0 - sigmoid)))
            back_ref[after, :] = low(grad_hidden * silu)
            return total + hidden * back

        return step

    zeros = jnp.zeros((UNIT_ROWS, tokens), WIDE)
    middle, last = expert_units // UNIT_ROWS, units // UNIT_ROWS
    expert_sum = lax.fori_loop(0, middle, unit_rows(combine), zeros)
    shared_sum = lax.fori_loop(middle, last, unit_rows(shared_gate), zeros)
    columns = pl.ds(half * tokens, tokens)
    start("out", hidden_ref, hidden_hbm.at[:, columns])
    start("out", back_ref, back_hbm.at[:, columns])
    expert_sum = jnp.sum(expert_sum, axis=0, keepdims=True)
    shared_sum = jnp.sum(shared_sum, axis=0, keepdims=True)
    sums = mine * expert_sum + jnp.where(places == 8, shared_sum, 0.0)
    sums = jnp.concatenate([sums, jnp.zeros((128 - sums.shape[0], tokens), WIDE)], axis=0)
    d_ref[:, width : width + 128] = low(sums.T)
    turned_ref[...] = back_ref[...].T
    step = width // 4

    def send(begin, size):
        for index in range(4):
            source = d_ref.at[block(index), pl.ds(begin, size)]
            start("out", source, d_hbm[index].at[:, pl.ds(begin, size)])

    for part in range(4):
        columns = slice(part * step, (part + 1) * step)
        d_ref[:, columns] = low(dot_plain(turned_ref[...], weight_ref[: 2 * units, columns]))
        send(part * step, step if part < 3 else step + 128)
    flat_ref[...] = hidden_ref[...].T
    for part in range(4):
        columns = slice(part * step, (part + 1) * step)
        begin = width + 128 + part * step
        d_ref[:, begin : begin + step] = low(
            dot_plain(flat_ref[...], weight_ref[2 * units :, columns])
        )
        send(begin, step)
    finish("out")


def units_forward_back(x_blocks, g_blocks, small_rows, mine, weights, earlier):
    rows, width = x_blocks[0].shape
    tokens = 4 * rows
    units = weights.shape[1] // 3
    vmem = pl.BlockSpec(memory_space=pltpu.VMEM)
    anywhere = pl.BlockSpec(memory_space=pl.ANY)
    return pl.pallas_call(
        functools.partial(units_kernel, len(earlier) // 2),
        in_specs=[anywhere] * 8 + [vmem] * 2 + [anywhere] * (1 + len(earlier)),
        out_specs=[anywhere] * 6,
        out_shape=[jax.ShapeDtypeStruct((rows, 2 * width + 128), LOW)] * 4
        + [
            jax.ShapeDtypeStruct((2 * units, 2 * tokens), LOW),
            jax.ShapeDtypeStruct((units, 2 * tokens), LOW),
        ],
        input_output_aliases={11 + index: 4 + index for index in range(len(earlier))},
        scratch_shapes=[
            pltpu.VMEM((3 * units, width), LOW),
            pltpu.VMEM((tokens, width), LOW),
            pltpu.VMEM((tokens, width), LOW),
            pltpu.VMEM((tokens, 128), LOW),
            pltpu.VMEM((units, tokens), WIDE),
            pltpu.VMEM((units, tokens), WIDE),
            pltpu.VMEM((units, tokens), WIDE),
            pltpu.VMEM((2 * units, tokens), LOW),
            pltpu.VMEM((units, tokens), LOW),
            pltpu.VMEM((tokens, 2 * units), LOW),
            pltpu.VMEM((tokens, units), LOW),
            pltpu.VMEM((tokens, 2 * width + 128), LOW),
            pltpu.SemaphoreType.DMA((70,)),
        ],
        compiler_params=params(),
        cost_estimate=estimate(11_000_000_000, 20_000_000),
        name="units",
    )(*x_blocks, *g_blocks, small_rows, mine, weights, *earlier)


def outer_kernel(*refs):
    back_ref, hidden_ref, x_refs, g_refs, out_ref = refs[0], refs[1], refs[2:10], refs[10:18], refs[18]
    units = hidden_ref.shape[0]
    rights = [jnp.concatenate([ref[...] for ref in part], axis=0) for part in (x_refs, g_refs)]
    back = low(dot_plain(back_ref[...], rights[0]))
    hidden = low(dot_plain(hidden_ref[...], rights[1]))
    for index in range(out_ref.shape[0]):
        columns = slice(index * 256, (index + 1) * 256)
        out_ref[index, : 2 * units] = back[:, columns]
        out_ref[index, 2 * units :] = hidden[:, columns]


def outer_products(back, hidden, x_blocks, g_blocks):
    units = hidden.shape[0]
    rows = x_blocks[0].shape[0]
    whole = lambda value: pl.BlockSpec(value.shape, lambda step: (0, 0))
    return pl.pallas_call(
        outer_kernel,
        grid=(4,),
        in_specs=[whole(back), whole(hidden)]
        + [pl.BlockSpec((rows, 512), lambda step: (0, step))] * 16,
        out_specs=pl.BlockSpec((2, 3 * units, 256), lambda step: (step, 0, 0)),
        out_shape=jax.ShapeDtypeStruct((8, 3 * units, 256), LOW),
        compiler_params=params(),
        cost_estimate=estimate(units * 2 * 1024 * 2048, 10_000_000),
        name="outer",
    )(back, hidden, *x_blocks, *g_blocks)


def pack_kernel(here_ref, qkv_ref, out_weight_ref, small_ref, out_ref):
    width, size = out_weight_ref.shape[1], qkv_ref.shape[2]
    out_ref[:, :width] = out_weight_ref[...]
    for index in range(3):
        out_ref[:, width + index * size : width + (index + 1) * size] = qkv_ref[index]
    out_ref[:, width + 3 * size :] = jnp.zeros_like(out_ref[:, width + 3 * size :])
    out_ref[: small_ref.shape[0], width + 3 * size :] = small_ref[...]


def pack_first(here, qkv, out_weight, small):
    shard, width = out_weight.shape
    return pl.pallas_call(
        pack_kernel,
        grid_spec=pltpu.PrefetchScalarGridSpec(
            num_scalar_prefetch=1,
            grid=(1,),
            in_specs=[
                pl.BlockSpec((3, shard, 128), lambda step, here_ref: (0, 0, here_ref[0])),
                pl.BlockSpec((shard, width), lambda step, here_ref: (0, 0)),
                pl.BlockSpec(small.shape, lambda step, here_ref: (0, 0)),
            ],
            out_specs=pl.BlockSpec((shard, width + 512), lambda step, here_ref: (0, 0)),
        ),
        out_shape=jax.ShapeDtypeStruct((shard, width + 512), LOW),
        cost_estimate=estimate(1000, 1000),
        name="pack",
    )(here, qkv, out_weight, small)


def branch_kernel(left_ref, weight_ref, out_ref):
    out_ref[...] = low(dot_rows(left_ref[...], weight_ref[...]))


def branch_part(attended, pack):
    rows, units = attended.shape
    width = pack.shape[0]
    return pl.pallas_call(
        branch_kernel,
        grid=(4,),
        in_specs=[
            pl.BlockSpec((rows, units), lambda step: (0, 0)),
            pl.BlockSpec((width // 4, units), lambda step: (step, 0)),
        ],
        out_specs=pl.BlockSpec((rows, width // 4), lambda step: (0, step)),
        out_shape=jax.ShapeDtypeStruct((rows, width), LOW),
        cost_estimate=estimate(600_000_000, 5_000_000),
        name="branch",
    )(attended, pack)


def branch_back_kernel(left_ref, weight_ref, out_ref):
    out_ref[...] = low(dot_plain(left_ref[...], weight_ref[...]))


def branch_back(grads, pack, units):
    rows, width = grads.shape
    return pl.pallas_call(
        branch_back_kernel,
        grid=(4,),
        in_specs=[
            pl.BlockSpec((rows, width), lambda step: (0, 0)),
            pl.BlockSpec((width, units // 4), lambda step: (0, step)),
        ],
        out_specs=pl.BlockSpec((rows, units // 4), lambda step: (0, step)),
        out_shape=jax.ShapeDtypeStruct((rows, units), LOW),
        cost_estimate=estimate(600_000_000, 5_000_000),
        name="branch_back",
    )(grads, pack)


def first_back_kernel(left_ref, weight_ref, out_ref):
    total = dot_rows(left_ref[0], weight_ref[0, 0])
    for part in (1, 2):
        total = total + dot_rows(left_ref[part], weight_ref[0, part])
    out_ref[...] = low(total)


def first_back(grads, weights):
    parts, rows, units = grads.shape
    shards, _, shard, _ = weights.shape
    return pl.pallas_call(
        first_back_kernel,
        grid=(shards,),
        in_specs=[
            pl.BlockSpec((parts, rows, units), lambda step: (0, 0, 0)),
            pl.BlockSpec((1, parts, shard, units), lambda step: (step, 0, 0, 0)),
        ],
        out_specs=pl.BlockSpec((rows, shard), lambda step: (0, step)),
        out_shape=jax.ShapeDtypeStruct((rows, shards * shard), LOW),
        cost_estimate=estimate(1_700_000_000, 13_000_000),
        name="first_back",
    )(grads, weights)


def place_kernel(places_ref, *refs):
    blocks = refs[:8]
    qkv_ref, out_ref, small_ref = refs[8:]
    for index, block in enumerate(blocks):
        columns = block_rows(places_ref[index], 128)
        for part in range(3):
            qkv_ref[part, :, columns] = wide(block[:, part * 128 : (part + 1) * 128])
        out_ref[:, columns] = wide(block[:, 512:640])
        small_ref[places_ref[index]] = wide(block[:, 384:512])


def place_last(places, blocks):
    shard = blocks[0].shape[0]
    vmem = pl.BlockSpec(memory_space=pltpu.VMEM)
    return pl.pallas_call(
        place_kernel,
        in_specs=[pl.BlockSpec(memory_space=pltpu.SMEM)] + [vmem] * 8,
        out_specs=[vmem] * 3,
        out_shape=(
            jax.ShapeDtypeStruct((3, shard, 1024), WIDE),
            jax.ShapeDtypeStruct((shard, 1024), WIDE),
            jax.ShapeDtypeStruct((8, shard, 128), WIDE),
        ),
        compiler_params=params(),
        cost_estimate=estimate(1000, 1000),
        name="place",
    )(places, *blocks)


def place_units_kernel(places_ref, *refs):
    blocks, (gate_ref, down_ref, shared_ref) = refs[:4], refs[-3:]
    expert_units = down_ref.shape[1]
    units = blocks[0].shape[0] // 3
    step = pl.program_id(0)
    for index, block in enumerate(blocks):

        @pl.when(step == index)
        def _(block=block):
            for part in range(3):
                start = part * units
                expert = wide(block[start : start + expert_units])
                if part < 2:
                    gate_ref[0, part] = expert
                else:
                    down_ref[0] = expert
                shared_ref[part, 0] = block[start + expert_units : start + units]


def place_units(places, blocks, expert_units, earlier):
    total, shard = blocks[0].shape
    shared_units = total // 3 - expert_units
    outs = (
        jax.ShapeDtypeStruct((8, 2, expert_units, shard), WIDE),
        jax.ShapeDtypeStruct((8, expert_units, shard), WIDE),
        jax.ShapeDtypeStruct((3, 8, shared_units, shard), LOW),
    )
    anywhere = pl.BlockSpec(memory_space=pl.ANY)
    return pl.pallas_call(
        place_units_kernel,
        grid_spec=pltpu.PrefetchScalarGridSpec(
            num_scalar_prefetch=1,
            grid=(4,),
            in_specs=[pl.BlockSpec((total, shard), lambda step, places_ref: (0, 0))] * 4
            + [anywhere] * len(earlier),
            out_specs=[
                pl.BlockSpec(
                    (1, 2, expert_units, shard),
                    lambda step, places_ref: (places_ref[step], 0, 0, 0),
                ),
                pl.BlockSpec(
                    (1, expert_units, shard),
                    lambda step, places_ref: (places_ref[step], 0, 0),
                ),
                pl.BlockSpec(
                    (3, 1, shared_units, shard),
                    lambda step, places_ref: (0, places_ref[step], 0, 0),
                ),
            ],
        ),
        out_shape=outs,
        input_output_aliases={5 + index: index for index in range(len(earlier))},
        compiler_params=params(),
        cost_estimate=estimate(1000, 1000),
        name="place_units",
    )(places, *blocks, *earlier)


def flip_kernel(one_ref, in_ref, gate_ref, down_ref):
    for part in range(2):
        gate_ref[:, part, :] = dot_rows(one_ref[...], in_ref[part])
    down_ref[...] = dot_rows(one_ref[...], in_ref[2])


def flip(values):
    parts, units, shard = values.shape
    return pl.pallas_call(
        flip_kernel,
        grid=(2,),
        in_specs=[
            pl.BlockSpec((shard, shard), lambda step: (0, 0)),
            pl.BlockSpec((parts, units // 2, shard), lambda step: (0, step, 0)),
        ],
        out_specs=[
            pl.BlockSpec((shard, 2, units // 2), lambda step: (0, 0, step)),
            pl.BlockSpec((shard, units // 2), lambda step: (0, step)),
        ],
        out_shape=(
            jax.ShapeDtypeStruct((shard, 2, units), WIDE),
            jax.ShapeDtypeStruct((shard, units), WIDE),
        ),
        compiler_params=params(),
        cost_estimate=estimate(1000, 1000),
        name="flip",
    )(jnp.eye(shard, dtype=LOW), values)


def after(values, earlier):
    return lax.optimization_barrier((values, earlier))[0]


def body(
    inputs,
    lengths,
    routes,
    norm_gains,
    w_qkv,
    b_qkv,
    w_o,
    w_router,
    w_sgate,
    w_sgu,
    w_sdown,
    w_egu,
    w_edown,
    grad_out,
):
    rows, width = inputs.shape
    shard = w_qkv.shape[0]
    experts = w_egu.shape[1]
    heads, bias_part = b_qkv.shape[1], b_qkv.shape[2]
    head_size = bias_part * 8
    expert_units = w_edown.shape[2]
    shared_units = w_sdown.shape[1] // 8
    units = expert_units + shared_units
    group, here = lax.axis_index("fsdp"), lax.axis_index("ctx")
    places = here * rows + jnp.arange(rows, dtype=jnp.int32)
    length_here = lax.dynamic_index_in_dim(lengths, group, 0, keepdims=False)
    valid = (places < length_here).astype(WIDE)[:, None]
    experts_range = jnp.arange(experts, dtype=jnp.int32)
    chosen = (
        jnp.any(routes[:, :, None] == experts_range[None, None, :], axis=1).astype(WIDE) * valid
    )
    block_places = jnp.stack(relative_places()).astype(jnp.int32)

    bias_here = lax.dynamic_slice(b_qkv, (0, here, 0), (3, 1, bias_part)).reshape(1, 3 * bias_part)
    small = jnp.concatenate(
        [
            w_router.T,
            w_sgate[None],
            norm_gains,
            jnp.pad(bias_here, ((0, 0), (0, shard - 3 * bias_part))),
            jnp.zeros((4, shard), LOW),
        ],
        axis=0,
    )
    first_pack = lax.all_gather(
        pack_first(
            here.astype(jnp.int32).reshape(1),
            w_qkv.transpose(1, 0, 2),
            w_o,
            small.reshape(32, 128),
        ),
        "fsdp",
        axis=0,
        tiled=True,
    )
    small_all = first_pack[:, 1408:].reshape(8, shard, 128)[:, :32].reshape(8, 16, shard)
    small_all = small_all.transpose(1, 0, 2)
    bias_all = small_all[11, :, : 3 * bias_part].reshape(8, 3, bias_part)
    bias_all = wide(bias_all.transpose(1, 0, 2).reshape(1, 3 * head_size))
    small_all = small_all.reshape(16, width)
    gain_first, gain_second = wide(small_all[9]), wide(small_all[10])
    gate_rows = small_all[: experts + 1]
    small_rows = jnp.pad(gate_rows, ((0, 16 - experts - 1), (0, 0)))
    x_first = gather_first(inputs)
    x_second = gather_second(x_first)
    grad_own = low(wide(grad_out) * valid)
    grad_pack = jnp.concatenate(
        [grad_own, jnp.pad(low(chosen), ((0, 0), (0, 128 - experts)))], axis=1
    )
    here_late = after(here, (x_first, x_second, grad_pack, block_places))
    shared_start = here_late * shared_units
    shared_gu = lax.dynamic_slice(w_sgu, (0, 0, shared_start), (shard, 2, shared_units))
    shared_gu = shared_gu.transpose(1, 2, 0)
    shared_down = lax.dynamic_slice(w_sdown, (0, shared_start), (shard, shared_units)).T
    expert_gu = lax.dynamic_index_in_dim(w_egu.transpose(1, 2, 3, 0), here_late, 0, keepdims=False)
    expert_down = lax.dynamic_index_in_dim(w_edown.transpose(1, 2, 0), here_late, 0, keepdims=False)
    unit_weights = lax.all_gather(
        jnp.concatenate(
            [expert_gu[0], shared_gu[0], expert_gu[1], shared_gu[1], expert_down, shared_down],
            axis=0,
        ),
        "fsdp",
        axis=0,
        tiled=False,
    )

    cosine, sine = rotary_tables(rows * 8, head_size)
    hidden_in = wide(inputs)
    x_blocks = gather_blocks(inputs, x_first, x_second)
    grad_pack = after(grad_pack, x_second)
    g_first = gather_first(grad_pack)
    g_second = gather_second(g_first)
    g_blocks = gather_blocks(grad_pack, g_first, g_second)
    queries, keys, values, attended, normed_first = attend(
        block_places, x_blocks, first_pack, gain_first[None], bias_all, cosine, sine
    )
    attended_own = lax.all_to_all(attended, "ctx", 0, 1, tiled=True)
    branch = add_halves(after(branch_part(attended_own, first_pack), g_first))
    middle = hidden_in + branch
    factor_second = inverse_rms(middle)
    normed_own = low(middle * factor_second * gain_second)

    n_first = gather_first(normed_own)
    n_second = gather_second(n_first)
    n_blocks = gather_blocks(normed_own, n_first, n_second)
    mine = (jnp.arange(16, dtype=jnp.int32) == here).astype(WIDE)[:, None]
    first_half, second_half = (0, 1, 2, 4), (3, 5, 6, 7)
    pick = lambda blocks, half: [blocks[index] for index in half]
    results = []
    for half in (first_half, second_half):
        results.append(
            units_forward_back(
                pick(n_blocks, half),
                pick(g_blocks, half),
                small_rows,
                mine,
                unit_weights,
                results[0][4:] if results else (),
            )
        )
    d_blocks = [None] * 8
    for half, result in zip((first_half, second_half), results):
        for place, index in enumerate(half):
            d_blocks[index] = result[place]
    back, hidden = results[1][4:]
    in_halves = lambda blocks: pick(blocks, first_half) + pick(blocks, second_half)
    weight_qkv_all = lax.all_gather(
        after(w_qkv.transpose(1, 0, 2), branch), "fsdp", axis=0, tiled=False
    )
    d_first = scatter_first(d_blocks)
    d_blocks[1:3] = after(d_blocks[1:3], (n_second, g_second))
    d_second = scatter_second(d_blocks, d_first)
    unit_part = outer_products(
        after(back, d_second[2:]),
        hidden,
        in_halves(n_blocks),
        in_halves(g_blocks),
    )
    unit_grads = lax.psum_scatter(unit_part, "fsdp", scatter_dimension=0, tiled=False)
    sums = scatter_sum(d_blocks[0], after(d_second, (unit_part, weight_qkv_all)))
    grad_sum = add_halves(sums[:, : width + 128])
    unit_first = large_first(unit_grads)

    logits = dot_rows(normed_own, gate_rows)
    probs_own = jax.nn.softmax(logits[:, :experts], axis=-1)
    gate_own = jax.nn.sigmoid(logits[:, experts : experts + 1])
    grad_normed, grad_combine = grad_sum[:, :width], grad_sum[:, width : width + experts]
    grad_gate = grad_sum[:, width + experts : width + experts + 1]
    picked = grad_combine * chosen
    grad_logits = low(
        probs_own * (picked - jnp.sum(picked * probs_own, axis=-1, keepdims=True))
    )
    grad_gate_logit = low(grad_gate * gate_own * (1.0 - gate_own))
    both = jnp.concatenate([grad_logits, grad_gate_logit], axis=1)
    grad_normed = grad_normed + dot_plain(both, gate_rows)
    grad_both = dot_columns(normed_own, both)
    grad_top = wide(grad_own)
    grad_gain_second = jnp.sum(grad_normed * middle * factor_second, axis=0)
    weighted = grad_normed * gain_second
    inner = jnp.mean(weighted * middle, axis=-1, keepdims=True)
    grad_middle = grad_top + weighted * factor_second - middle * factor_second**3 * inner
    grad_branch = low(grad_middle)

    grad_attended = branch_back(grad_branch, first_pack, heads * head_size)
    grad_heads = lax.all_to_all(
        grad_attended.reshape(rows, heads, head_size).transpose(1, 0, 2), "ctx", 0, 0, tiled=True
    ).reshape(rows * 8, head_size)
    grad_heads = after(grad_heads, unit_first)
    unit_second = large_second(unit_first)
    mixed = add_halves(after(sums[:, width + 128 :], grad_heads))
    result = low(valid * (middle + mixed))
    out_part = lax.psum_scatter(
        low(dot_columns(grad_branch, attended_own)), "fsdp", scatter_dimension=0, tiled=True
    )
    grad_proj, grad_bias = attend_back(queries, keys, values, grad_heads, cosine, sine)
    out_parts = out_part.reshape(shard, heads, head_size).transpose(1, 0, 2)
    out_parts = lax.all_to_all(after(out_parts, grad_proj), "ctx", 0, 0, tiled=True)
    grad_w_o_here = low(jnp.sum(wide(out_parts), axis=0))
    proj_own = lax.all_to_all(
        grad_proj.reshape(8, rows, 3 * head_size), "ctx", 0, 0, tiled=True
    )
    grad_qkv_here = low(dot_columns(normed_first, grad_proj))
    bias_rows = grad_bias.reshape(3, 8, bias_part).transpose(1, 0, 2).reshape(8, 3 * bias_part)
    bias_rows = jnp.pad(bias_rows, ((0, 0), (0, shard - 3 * bias_part))).reshape(width, 1)
    small_grads = low(jnp.concatenate([grad_both, grad_gain_second[:, None], bias_rows], axis=1))
    small_grads = jnp.pad(small_grads, ((0, 0), (0, 128 - small_grads.shape[1])))
    last_part = jnp.concatenate([grad_qkv_here, small_grads], axis=1)
    proj_own = after(proj_own, (last_part, unit_second, grad_w_o_here))
    proj_own = proj_own.reshape(8, rows, 3, head_size).transpose(2, 1, 0, 3)
    proj_own = proj_own.reshape(3, rows, heads * head_size)
    first_part = first_back(proj_own, weight_qkv_all)
    last_pack = lax.psum_scatter(last_part, "fsdp", scatter_dimension=0, tiled=True)
    weights_here = lax.dynamic_slice(
        w_qkv, (0, 0, here * head_size), (shard, 3, head_size)
    ).reshape(shard, 3 * head_size)
    products = jnp.sum(wide(weights_here) * wide(last_pack[:, : 3 * head_size]), axis=1)
    products = products + lax.ppermute(products, "tp", [(0, 1), (1, 0)])
    spare = 3 * head_size + experts + 3
    last_block = (
        jnp.concatenate(
            [
                last_pack[:, :spare],
                low(products)[:, None],
                last_pack[:, spare + 1 :],
                grad_w_o_here,
            ],
            axis=1,
        )
    )
    last_first = gather_first(last_block)
    unit_third = large_third(unit_second)
    grad_first = after(add_halves(after(first_part, last_first)), (result, unit_third))
    last_blocks = gather_blocks(last_block, last_first, gather_second(last_first))
    factor_first = inverse_rms(hidden_in)
    weighted = grad_first * gain_first
    inner = jnp.mean(weighted * hidden_in, axis=-1, keepdims=True)
    grad_input = grad_middle + weighted * factor_first - hidden_in * factor_first**3 * inner

    unit_blocks = large_blocks(unit_grads, unit_first, unit_second, unit_third)
    early, late = (0, 1, 2, 4), (3, 5, 6, 7)
    placed = ()
    for half in (early, late):
        block_half = after(block_places, unit_second)[jnp.array(half)]
        placed = place_units(block_half, pick(unit_blocks, half), expert_units, placed)
    grad_egu, grad_edown, shared_grads = placed
    grad_w_sgu, grad_w_sdown = flip(shared_grads.reshape(3, 8 * shared_units, shard))
    grad_qkv, grad_w_o, small_sums = place_last(block_places, last_blocks)
    grad_w_qkv = grad_qkv.transpose(1, 0, 2)
    summed = jnp.sum(small_sums[:, :, : experts + 4], axis=0)
    grad_b_qkv = (
        small_sums[:, : 3 * bias_part, experts + 2].reshape(8, 3, bias_part).transpose(1, 0, 2)
    )
    grad_gain_first = summed[:, experts + 3] / wide(norm_gains[0])
    return (
        result,
        low(grad_input),
        jnp.stack([grad_gain_first, summed[:, experts + 1]]),
        grad_w_qkv,
        grad_b_qkv,
        grad_w_o,
        summed[:, :experts],
        summed[:, experts],
        grad_w_sgu,
        grad_w_sdown,
        grad_egu.transpose(3, 0, 1, 2),
        grad_edown.transpose(2, 0, 1),
    )


def solution(mesh):
    return jax.shard_map(
        body,
        mesh=mesh,
        in_specs=(
            P(("fsdp", "ctx"), None),
            P(),
            P(("fsdp", "ctx"), None),
            P(None, "fsdp"),
            P("fsdp", None, "tp"),
            P(None, "tp", "fsdp"),
            P("fsdp", "tp"),
            P("fsdp", None),
            P("fsdp"),
            P("fsdp", None, "tp"),
            P("fsdp", "tp"),
            P("fsdp", None, None, "tp"),
            P("fsdp", None, "tp"),
            P(("fsdp", "ctx"), None),
        ),
        out_specs=(
            P(("fsdp", "ctx"), None),
            P(("fsdp", "ctx"), None),
            P(None, "fsdp"),
            P("fsdp", None, "tp"),
            P(None, "tp", "fsdp"),
            P("fsdp", "tp"),
            P("fsdp", None),
            P("fsdp"),
            P("fsdp", None, "tp"),
            P("fsdp", "tp"),
            P("fsdp", None, None, "tp"),
            P("fsdp", None, "tp"),
        ),
        check_vma=False,
    )
```

```python
import functools

import jax
import jax.numpy as jnp
import numpy as np
from jax import lax
from jax.experimental import pallas as pl
from jax.experimental.pallas import tpu as pltpu
from jax.sharding import PartitionSpec as P

EPSILON = 1e-06
ROPE_BASE = 1000000.0
MASKED_SCORE = -1e30
LOW = jnp.bfloat16
WIDE = jnp.float32
VMEM_BYTES = 56 * 1024 * 1024


def low(values):
    return values.astype(LOW)


def wide(values):
    return values.astype(WIDE)


def rotary_tables(row_count, head_size):
    middle = head_size // 2
    powers = -(np.arange(middle, dtype=np.float32) * np.float32(2.0)) / np.float32(head_size)
    inverse = np.power(np.float32(ROPE_BASE), powers).astype(np.float32)
    places = np.arange(row_count, dtype=np.float32)
    angles = (places[:, None] * inverse[None, :]).astype(np.float32)
    cosine, sine = np.cos(angles), np.sin(angles)
    return (
        jnp.asarray(np.concatenate([cosine, cosine], axis=-1)),
        jnp.asarray(np.concatenate([-sine, sine], axis=-1)),
    )


def inverse_rms(values):
    return lax.rsqrt(jnp.mean(values * values, axis=-1, keepdims=True) + EPSILON)


def ring(step):
    return [(i, (i + step) % 8) for i in range(8)]


PAIR = [(i, i ^ 1) for i in range(8)]


def up(values):
    return lax.ppermute(values, "ctx", ring(2))


def down(values):
    return lax.ppermute(values, "ctx", ring(-2))


def swap(values):
    return lax.ppermute(values, "ctx", PAIR)


def relative_places():
    here = lax.axis_index("ctx")
    return [(here + step) % 8 for step in (0, 6, 2, 4)] + [
        ((here ^ 1) + step) % 8 for step in (0, 6, 2, 4)
    ]


def across(values):
    return lax.ppermute(values, "ctx", ring(4))


def gather_first(block):
    return up(block), down(block), swap(block), across(block)


def gather_second(first):
    _, _, pair, opposite = first
    return up(pair), down(pair), swap(opposite)


def gather_blocks(block, first, second):
    left, right, pair, opposite = first
    return [block, left, right, opposite, pair, *second]


def gather_relative(block):
    first = gather_first(block)
    return gather_blocks(block, first, gather_second(first))


def large_first(block):
    return up(block), down(block), swap(block)


def large_second(first):
    left, right, pair = first
    half = left.shape[0] // 2
    return up(left[:half]), down(right[half:]), up(pair), down(pair)


def large_third(second):
    _, _, pair_left, pair_right = second
    half = pair_left.shape[0] // 2
    return up(pair_left[:half]), down(pair_right[half:])


def large_blocks(block, first, second, third):
    left, right, pair = first
    opposite = jnp.concatenate(second[:2], axis=0)
    pair_opposite = jnp.concatenate(third, axis=0)
    return [block, left, right, opposite, pair, second[2], second[3], pair_opposite]


def scatter_first(blocks):
    _, _, _, _, _, pair_left, pair_right, pair_opposite = blocks
    return swap(low(pair_opposite)), up(low(pair_right)), down(low(pair_left))


def scatter_second(blocks, first):
    _, left, right, opposite, pair, _, _, _ = blocks
    from_pair, pair_up, pair_down = first
    return (
        across(low(wide(opposite) + wide(from_pair))),
        swap(low(wide(pair) + wide(pair_up) + wide(pair_down))),
        up(low(right)),
        down(low(left)),
    )


def scatter_sum(own, second):
    far, crossing, last_up, last_down = second
    return wide(own) + wide(far) + wide(crossing) + wide(last_up) + wide(last_down)


def scatter_relative(blocks):
    return scatter_sum(blocks[0], scatter_second(blocks, scatter_first(blocks)))


def add_halves(values):
    mine = low(values)
    return wide(mine) + wide(lax.ppermute(mine, "tp", [(0, 1), (1, 0)]))


QUERY_ROWS = 256


def estimate(flops, bytes_accessed):
    return pl.CostEstimate(
        flops=flops // 1000, bytes_accessed=bytes_accessed // 1000, transcendentals=0
    )


def params():
    return pltpu.CompilerParams(vmem_limit_bytes=VMEM_BYTES)


def turn(values, cosine, sine):
    return values * cosine + pltpu.roll(values, values.shape[-1] // 2, 1) * sine


def dot_plain(left, right):
    return jnp.dot(left, right, preferred_element_type=WIDE)


def dot_rows(left, right):
    return lax.dot_general(left, right, (((1,), (1,)), ((), ())), preferred_element_type=WIDE)


def dot_columns(left, right):
    return lax.dot_general(left, right, (((0,), (0,)), ((), ())), preferred_element_type=WIDE)


def probabilities(queries, keys, start, scale):
    scores = dot_rows(queries, keys) * scale
    rows = start + lax.broadcasted_iota(jnp.int32, scores.shape, 0)
    columns = lax.broadcasted_iota(jnp.int32, scores.shape, 1)
    scores = jnp.where(columns <= rows, scores, MASKED_SCORE)
    expons = jnp.exp(scores - jnp.max(scores, axis=-1, keepdims=True))
    return expons * (1.0 / jnp.sum(expons, axis=-1, keepdims=True))


def block_rows(place, rows):
    return pl.ds(pl.multiple_of(place * rows, rows), rows)


def attend_kernel(places_ref, *refs):
    blocks = refs[:8]
    weight_ref, gain_ref, bias_ref, cos_ref, sin_ref = refs[8:13]
    q_ref, k_ref, v_ref, out_ref, normed_ref = refs[13:]
    size = cos_ref.shape[1]
    scale = size ** (-0.5)
    gain = gain_ref[...]
    for index, block in enumerate(blocks):
        values = wide(block[...])
        normed = low(values * inverse_rms(values) * gain)
        normed_ref[block_rows(places_ref[index], block.shape[0]), :] = normed
    for start in range(0, q_ref.shape[0], QUERY_ROWS):
        end = start + QUERY_ROWS
        proj = dot_plain(normed_ref[start:end], weight_ref[:, : 3 * size]) + bias_ref[...]
        cosine, sine = cos_ref[start:end], sin_ref[start:end]
        q_ref[start:end] = low(turn(proj[:, :size], cosine, sine))
        k_ref[start:end] = low(turn(proj[:, size : 2 * size], cosine, sine))
        v_ref[start:end] = low(proj[:, 2 * size :])
    for start in range(0, q_ref.shape[0], QUERY_ROWS):
        end = start + QUERY_ROWS
        probs = low(probabilities(q_ref[start:end], k_ref[:end], start, scale))
        out_ref[start:end] = low(dot_plain(probs, v_ref[:end]))


def attend(places, blocks, pack, gain, bias, cosine, sine):
    rows, size = cosine.shape
    width = blocks[0].shape[1]
    one = jax.ShapeDtypeStruct((rows, size), LOW)
    whole = pl.BlockSpec(memory_space=pltpu.VMEM)
    part = pl.BlockSpec((width, 512), lambda step: (0, 2))
    whole_of = lambda shape: pl.BlockSpec(shape, lambda step: (0, 0))
    return pl.pallas_call(
        attend_kernel,
        grid=(1,),
        in_specs=[pl.BlockSpec(memory_space=pltpu.SMEM)]
        + [whole_of(block.shape) for block in blocks]
        + [part]
        + [whole_of(value.shape) for value in (gain, bias, cosine, sine)],
        out_specs=[whole_of((rows, size))] * 4 + [whole_of((rows, width))],
        out_shape=(one, one, one, one, jax.ShapeDtypeStruct((rows, width), LOW)),
        compiler_params=params(),
        cost_estimate=estimate(9_000_000_000, 12_000_000),
        name="attend",
    )(places, *blocks, pack, gain, bias, cosine, sine)


def attend_back_kernel(
    q_ref, k_ref, v_ref, grad_ref, cos_ref, sin_ref, out_ref, bias_ref, dk_ref, dv_ref
):
    size = cos_ref.shape[1]
    scale = size ** (-0.5)
    dk_ref[...] = jnp.zeros_like(dk_ref)
    dv_ref[...] = jnp.zeros_like(dv_ref)
    bias = jnp.zeros((1, size), WIDE)
    for start in range(0, q_ref.shape[0], QUERY_ROWS):
        end = start + QUERY_ROWS
        queries, grads = q_ref[start:end], grad_ref[start:end]
        probs = probabilities(queries, k_ref[:end], start, scale)
        grad_probs = dot_rows(grads, v_ref[:end])
        inner = jnp.sum(probs * grad_probs, axis=-1, keepdims=True)
        grad_scores = low(probs * (grad_probs - inner))
        grad_queries = dot_plain(grad_scores, k_ref[:end]) * scale
        grad_queries = low(turn(grad_queries, cos_ref[start:end], -sin_ref[start:end]))
        out_ref[start:end, :size] = grad_queries
        bias = bias + jnp.sum(wide(grad_queries), axis=0, keepdims=True)
        dk_ref[:end] += dot_columns(grad_scores, queries) * scale
        dv_ref[:end] += dot_columns(low(probs), grads)
    bias_ref[:, :size] = bias
    grad_keys = low(turn(dk_ref[...], cos_ref[...], -sin_ref[...]))
    out_ref[:, size : 2 * size] = grad_keys
    bias_ref[:, size : 2 * size] = jnp.sum(wide(grad_keys), axis=0, keepdims=True)
    grad_values = low(dv_ref[...])
    out_ref[:, 2 * size :] = grad_values
    bias_ref[:, 2 * size :] = jnp.sum(wide(grad_values), axis=0, keepdims=True)


def attend_back(queries, keys, values, grads, cosine, sine):
    rows, size = cosine.shape
    return pl.pallas_call(
        attend_back_kernel,
        out_shape=(
            jax.ShapeDtypeStruct((rows, 3 * size), LOW),
            jax.ShapeDtypeStruct((1, 3 * size), WIDE),
        ),
        scratch_shapes=[pltpu.VMEM((rows, size), WIDE), pltpu.VMEM((rows, size), WIDE)],
        compiler_params=params(),
        cost_estimate=estimate(7_000_000_000, 6_000_000),
        name="attend_back",
    )(queries, keys, values, grads, cosine, sine)


UNIT_ROWS = 16


def units_kernel(half, *refs):
    x_hbm, g_hbm = refs[:4], refs[4:8]
    small_ref, mine_ref, weight_hbm = refs[8:11]
    refs = refs[:11] + refs[11 + 2 * half :]
    d_hbm, back_hbm, hidden_hbm = refs[11:15], refs[15], refs[16]
    weight_ref, x_ref, g_ref, tail_ref, gate_ref, up_ref, down_ref = refs[17:24]
    back_ref, hidden_ref, turned_ref, flat_ref, d_ref, sems = refs[24:]
    units, tokens = hidden_ref.shape
    rows, width = x_hbm[0].shape
    expert_units = units * 2 // 3
    count = 0
    started = {}

    def start(name, source, target):
        nonlocal count
        copy = pltpu.make_async_copy(source, target, sems.at[count])
        copy.start()
        count += 1
        started.setdefault(name, []).append(copy)

    def finish(name):
        for copy in started[name]:
            copy.wait()

    def start_weights(part):
        group = pl.ds(part * units, units)
        for index in range(8):
            columns = pl.ds(index * (width // 8), width // 8)
            start(part, weight_hbm.at[index, group, :], weight_ref.at[group, columns])

    block = lambda index: pl.ds(index * rows, rows)
    for index in range(4):
        start("x", x_hbm[index], x_ref.at[block(index)])
    start_weights(0)
    start_weights(1)
    for index in range(4):
        start("tail", g_hbm[index].at[:, pl.ds(width, 128)], tail_ref.at[block(index)])
        start("g", g_hbm[index].at[:, pl.ds(0, width)], g_ref.at[block(index)])
    start_weights(2)
    finish("x")
    logits = dot_rows(small_ref[...], x_ref[...])
    places = lax.broadcasted_iota(jnp.int32, logits.shape, 0)
    routed = jnp.where(places < 8, logits, MASKED_SCORE)
    expons = jnp.exp(routed - jnp.max(routed, axis=0, keepdims=True))
    probs = expons / jnp.sum(expons, axis=0, keepdims=True)
    shared_gate = jax.nn.sigmoid(
        jnp.sum(jnp.where(places == 8, logits, 0.0), axis=0, keepdims=True)
    )
    for part, (target, source) in enumerate(((gate_ref, x_ref), (up_ref, x_ref), (down_ref, g_ref))):
        if part == 2:
            finish("g")
        finish(part)
        target[...] = dot_rows(weight_ref[part * units : (part + 1) * units], source[...])
    finish("tail")
    chosen = wide(tail_ref[...]).T[: places.shape[0]]
    mine = mine_ref[...]
    combine = jnp.sum(probs * chosen * mine, axis=0, keepdims=True)

    def unit_rows(scale):
        def step(index, total):
            chunk = pl.ds(pl.multiple_of(index * UNIT_ROWS, UNIT_ROWS), UNIT_ROWS)
            after = pl.ds(pl.multiple_of(units + index * UNIT_ROWS, UNIT_ROWS), UNIT_ROWS)
            gate, upper, back = gate_ref[chunk, :], up_ref[chunk, :], down_ref[chunk, :]
            sigmoid = jax.nn.sigmoid(gate)
            silu = gate * sigmoid
            hidden = silu * upper
            hidden_ref[chunk, :] = low(hidden * scale)
            grad_hidden = back * scale
            back_ref[chunk, :] = low(grad_hidden * upper * (sigmoid + silu * (1.0 - sigmoid)))
            back_ref[after, :] = low(grad_hidden * silu)
            return total + hidden * back

        return step

    zeros = jnp.zeros((UNIT_ROWS, tokens), WIDE)
    middle, last = expert_units // UNIT_ROWS, units // UNIT_ROWS
    expert_sum = lax.fori_loop(0, middle, unit_rows(combine), zeros)
    shared_sum = lax.fori_loop(middle, last, unit_rows(shared_gate), zeros)
    columns = pl.ds(half * tokens, tokens)
    start("out", hidden_ref, hidden_hbm.at[:, columns])
    start("out", back_ref, back_hbm.at[:, columns])
    expert_sum = jnp.sum(expert_sum, axis=0, keepdims=True)
    shared_sum = jnp.sum(shared_sum, axis=0, keepdims=True)
    sums = mine * expert_sum + jnp.where(places == 8, shared_sum, 0.0)
    sums = jnp.concatenate([sums, jnp.zeros((128 - sums.shape[0], tokens), WIDE)], axis=0)
    d_ref[:, width : width + 128] = low(sums.T)
    turned_ref[...] = back_ref[...].T
    step = width // 4

    def send(begin, size):
        for index in range(4):
            source = d_ref.at[block(index), pl.ds(begin, size)]
            start("out", source, d_hbm[index].at[:, pl.ds(begin, size)])

    for part in range(4):
        columns = slice(part * step, (part + 1) * step)
        d_ref[:, columns] = low(dot_plain(turned_ref[...], weight_ref[: 2 * units, columns]))
        send(part * step, step if part < 3 else step + 128)
    flat_ref[...] = hidden_ref[...].T
    for part in range(4):
        columns = slice(part * step, (part + 1) * step)
        begin = width + 128 + part * step
        d_ref[:, begin : begin + step] = low(
            dot_plain(flat_ref[...], weight_ref[2 * units :, columns])
        )
        send(begin, step)
    finish("out")


def units_forward_back(x_blocks, g_blocks, small_rows, mine, weights, earlier):
    rows, width = x_blocks[0].shape
    tokens = 4 * rows
    units = weights.shape[1] // 3
    vmem = pl.BlockSpec(memory_space=pltpu.VMEM)
    anywhere = pl.BlockSpec(memory_space=pl.ANY)
    return pl.pallas_call(
        functools.partial(units_kernel, len(earlier) // 2),
        in_specs=[anywhere] * 8 + [vmem] * 2 + [anywhere] * (1 + len(earlier)),
        out_specs=[anywhere] * 6,
        out_shape=[jax.ShapeDtypeStruct((rows, 2 * width + 128), LOW)] * 4
        + [
            jax.ShapeDtypeStruct((2 * units, 2 * tokens), LOW),
            jax.ShapeDtypeStruct((units, 2 * tokens), LOW),
        ],
        input_output_aliases={11 + index: 4 + index for index in range(len(earlier))},
        scratch_shapes=[
            pltpu.VMEM((3 * units, width), LOW),
            pltpu.VMEM((tokens, width), LOW),
            pltpu.VMEM((tokens, width), LOW),
            pltpu.VMEM((tokens, 128), LOW),
            pltpu.VMEM((units, tokens), WIDE),
            pltpu.VMEM((units, tokens), WIDE),
            pltpu.VMEM((units, tokens), WIDE),
            pltpu.VMEM((2 * units, tokens), LOW),
            pltpu.VMEM((units, tokens), LOW),
            pltpu.VMEM((tokens, 2 * units), LOW),
            pltpu.VMEM((tokens, units), LOW),
            pltpu.VMEM((tokens, 2 * width + 128), LOW),
            pltpu.SemaphoreType.DMA((70,)),
        ],
        compiler_params=params(),
        cost_estimate=estimate(11_000_000_000, 20_000_000),
        name="units",
    )(*x_blocks, *g_blocks, small_rows, mine, weights, *earlier)


def outer_kernel(*refs):
    back_ref, hidden_ref, x_refs, g_refs, out_ref = refs[0], refs[1], refs[2:10], refs[10:18], refs[18]
    units = hidden_ref.shape[0]
    rights = [jnp.concatenate([ref[...] for ref in part], axis=0) for part in (x_refs, g_refs)]
    back = low(dot_plain(back_ref[...], rights[0]))
    hidden = low(dot_plain(hidden_ref[...], rights[1]))
    for index in range(out_ref.shape[0]):
        columns = slice(index * 256, (index + 1) * 256)
        out_ref[index, : 2 * units] = back[:, columns]
        out_ref[index, 2 * units :] = hidden[:, columns]


def outer_products(back, hidden, x_blocks, g_blocks):
    units = hidden.shape[0]
    rows = x_blocks[0].shape[0]
    whole = lambda value: pl.BlockSpec(value.shape, lambda step: (0, 0))
    return pl.pallas_call(
        outer_kernel,
        grid=(4,),
        in_specs=[whole(back), whole(hidden)]
        + [pl.BlockSpec((rows, 512), lambda step: (0, step))] * 16,
        out_specs=pl.BlockSpec((2, 3 * units, 256), lambda step: (step, 0, 0)),
        out_shape=jax.ShapeDtypeStruct((8, 3 * units, 256), LOW),
        compiler_params=params(),
        cost_estimate=estimate(units * 2 * 1024 * 2048, 10_000_000),
        name="outer",
    )(back, hidden, *x_blocks, *g_blocks)


def pack_kernel(here_ref, qkv_ref, out_weight_ref, small_ref, out_ref):
    width, size = out_weight_ref.shape[1], qkv_ref.shape[2]
    out_ref[:, :width] = out_weight_ref[...]
    for index in range(3):
        out_ref[:, width + index * size : width + (index + 1) * size] = qkv_ref[index]
    out_ref[:, width + 3 * size :] = jnp.zeros_like(out_ref[:, width + 3 * size :])
    out_ref[: small_ref.shape[0], width + 3 * size :] = small_ref[...]


def pack_first(here, qkv, out_weight, small):
    shard, width = out_weight.shape
    return pl.pallas_call(
        pack_kernel,
        grid_spec=pltpu.PrefetchScalarGridSpec(
            num_scalar_prefetch=1,
            grid=(1,),
            in_specs=[
                pl.BlockSpec((3, shard, 128), lambda step, here_ref: (0, 0, here_ref[0])),
                pl.BlockSpec((shard, width), lambda step, here_ref: (0, 0)),
                pl.BlockSpec(small.shape, lambda step, here_ref: (0, 0)),
            ],
            out_specs=pl.BlockSpec((shard, width + 512), lambda step, here_ref: (0, 0)),
        ),
        out_shape=jax.ShapeDtypeStruct((shard, width + 512), LOW),
        cost_estimate=estimate(1000, 1000),
        name="pack",
    )(here, qkv, out_weight, small)


def branch_kernel(left_ref, weight_ref, out_ref):
    out_ref[...] = low(dot_rows(left_ref[...], weight_ref[...]))


def branch_part(attended, pack):
    rows, units = attended.shape
    width = pack.shape[0]
    return pl.pallas_call(
        branch_kernel,
        grid=(4,),
        in_specs=[
            pl.BlockSpec((rows, units), lambda step: (0, 0)),
            pl.BlockSpec((width // 4, units), lambda step: (step, 0)),
        ],
        out_specs=pl.BlockSpec((rows, width // 4), lambda step: (0, step)),
        out_shape=jax.ShapeDtypeStruct((rows, width), LOW),
        cost_estimate=estimate(600_000_000, 5_000_000),
        name="branch",
    )(attended, pack)


def branch_back_kernel(left_ref, weight_ref, out_ref):
    out_ref[...] = low(dot_plain(left_ref[...], weight_ref[...]))


def branch_back(grads, pack, units):
    rows, width = grads.shape
    return pl.pallas_call(
        branch_back_kernel,
        grid=(4,),
        in_specs=[
            pl.BlockSpec((rows, width), lambda step: (0, 0)),
            pl.BlockSpec((width, units // 4), lambda step: (0, step)),
        ],
        out_specs=pl.BlockSpec((rows, units // 4), lambda step: (0, step)),
        out_shape=jax.ShapeDtypeStruct((rows, units), LOW),
        cost_estimate=estimate(600_000_000, 5_000_000),
        name="branch_back",
    )(grads, pack)


def first_back_kernel(left_ref, weight_ref, out_ref):
    total = dot_rows(left_ref[0], weight_ref[0, 0])
    for part in (1, 2):
        total = total + dot_rows(left_ref[part], weight_ref[0, part])
    out_ref[...] = low(total)


def first_back(grads, weights):
    parts, rows, units = grads.shape
    shards, _, shard, _ = weights.shape
    return pl.pallas_call(
        first_back_kernel,
        grid=(shards,),
        in_specs=[
            pl.BlockSpec((parts, rows, units), lambda step: (0, 0, 0)),
            pl.BlockSpec((1, parts, shard, units), lambda step: (step, 0, 0, 0)),
        ],
        out_specs=pl.BlockSpec((rows, shard), lambda step: (0, step)),
        out_shape=jax.ShapeDtypeStruct((rows, shards * shard), LOW),
        cost_estimate=estimate(1_700_000_000, 13_000_000),
        name="first_back",
    )(grads, weights)


def place_kernel(places_ref, *refs):
    blocks = refs[:8]
    qkv_ref, out_ref, small_ref = refs[8:]
    for index, block in enumerate(blocks):
        columns = block_rows(places_ref[index], 128)
        for part in range(3):
            qkv_ref[part, :, columns] = wide(block[:, part * 128 : (part + 1) * 128])
        out_ref[:, columns] = wide(block[:, 512:640])
        small_ref[places_ref[index]] = wide(block[:, 384:512])


def place_last(places, blocks):
    shard = blocks[0].shape[0]
    vmem = pl.BlockSpec(memory_space=pltpu.VMEM)
    return pl.pallas_call(
        place_kernel,
        in_specs=[pl.BlockSpec(memory_space=pltpu.SMEM)] + [vmem] * 8,
        out_specs=[vmem] * 3,
        out_shape=(
            jax.ShapeDtypeStruct((3, shard, 1024), WIDE),
            jax.ShapeDtypeStruct((shard, 1024), WIDE),
            jax.ShapeDtypeStruct((8, shard, 128), WIDE),
        ),
        compiler_params=params(),
        cost_estimate=estimate(1000, 1000),
        name="place",
    )(places, *blocks)


def place_units_kernel(places_ref, *refs):
    blocks, (gate_ref, down_ref, shared_ref) = refs[:4], refs[-3:]
    expert_units = down_ref.shape[1]
    units = blocks[0].shape[0] // 3
    step = pl.program_id(0)
    for index, block in enumerate(blocks):

        @pl.when(step == index)
        def _(block=block):
            for part in range(3):
                start = part * units
                expert = wide(block[start : start + expert_units])
                if part < 2:
                    gate_ref[0, part] = expert
                else:
                    down_ref[0] = expert
                shared_ref[part, 0] = block[start + expert_units : start + units]


def place_units(places, blocks, expert_units, earlier):
    total, shard = blocks[0].shape
    shared_units = total // 3 - expert_units
    outs = (
        jax.ShapeDtypeStruct((8, 2, expert_units, shard), WIDE),
        jax.ShapeDtypeStruct((8, expert_units, shard), WIDE),
        jax.ShapeDtypeStruct((3, 8, shared_units, shard), LOW),
    )
    anywhere = pl.BlockSpec(memory_space=pl.ANY)
    return pl.pallas_call(
        place_units_kernel,
        grid_spec=pltpu.PrefetchScalarGridSpec(
            num_scalar_prefetch=1,
            grid=(4,),
            in_specs=[pl.BlockSpec((total, shard), lambda step, places_ref: (0, 0))] * 4
            + [anywhere] * len(earlier),
            out_specs=[
                pl.BlockSpec(
                    (1, 2, expert_units, shard),
                    lambda step, places_ref: (places_ref[step], 0, 0, 0),
                ),
                pl.BlockSpec(
                    (1, expert_units, shard),
                    lambda step, places_ref: (places_ref[step], 0, 0),
                ),
                pl.BlockSpec(
                    (3, 1, shared_units, shard),
                    lambda step, places_ref: (0, places_ref[step], 0, 0),
                ),
            ],
        ),
        out_shape=outs,
        input_output_aliases={5 + index: index for index in range(len(earlier))},
        compiler_params=params(),
        cost_estimate=estimate(1000, 1000),
        name="place_units",
    )(places, *blocks, *earlier)


def flip_kernel(one_ref, in_ref, gate_ref, down_ref):
    for part in range(2):
        gate_ref[:, part, :] = dot_rows(one_ref[...], in_ref[part])
    down_ref[...] = dot_rows(one_ref[...], in_ref[2])


def flip(values):
    parts, units, shard = values.shape
    return pl.pallas_call(
        flip_kernel,
        grid=(2,),
        in_specs=[
            pl.BlockSpec((shard, shard), lambda step: (0, 0)),
            pl.BlockSpec((parts, units // 2, shard), lambda step: (0, step, 0)),
        ],
        out_specs=[
            pl.BlockSpec((shard, 2, units // 2), lambda step: (0, 0, step)),
            pl.BlockSpec((shard, units // 2), lambda step: (0, step)),
        ],
        out_shape=(
            jax.ShapeDtypeStruct((shard, 2, units), WIDE),
            jax.ShapeDtypeStruct((shard, units), WIDE),
        ),
        compiler_params=params(),
        cost_estimate=estimate(1000, 1000),
        name="flip",
    )(jnp.eye(shard, dtype=LOW), values)


def after(values, earlier):
    return lax.optimization_barrier((values, earlier))[0]


def body(
    inputs,
    lengths,
    routes,
    norm_gains,
    w_qkv,
    b_qkv,
    w_o,
    w_router,
    w_sgate,
    w_sgu,
    w_sdown,
    w_egu,
    w_edown,
    grad_out,
):
    rows, width = inputs.shape
    shard = w_qkv.shape[0]
    experts = w_egu.shape[1]
    heads, bias_part = b_qkv.shape[1], b_qkv.shape[2]
    head_size = bias_part * 8
    expert_units = w_edown.shape[2]
    shared_units = w_sdown.shape[1] // 8
    units = expert_units + shared_units
    group, here = lax.axis_index("fsdp"), lax.axis_index("ctx")
    places = here * rows + jnp.arange(rows, dtype=jnp.int32)
    length_here = lax.dynamic_index_in_dim(lengths, group, 0, keepdims=False)
    valid = (places < length_here).astype(WIDE)[:, None]
    experts_range = jnp.arange(experts, dtype=jnp.int32)
    chosen = (
        jnp.any(routes[:, :, None] == experts_range[None, None, :], axis=1).astype(WIDE) * valid
    )
    block_places = jnp.stack(relative_places()).astype(jnp.int32)

    bias_here = lax.dynamic_slice(b_qkv, (0, here, 0), (3, 1, bias_part)).reshape(1, 3 * bias_part)
    small = jnp.concatenate(
        [
            w_router.T,
            w_sgate[None],
            norm_gains,
            jnp.pad(bias_here, ((0, 0), (0, shard - 3 * bias_part))),
            jnp.zeros((4, shard), LOW),
        ],
        axis=0,
    )
    first_pack = lax.all_gather(
        pack_first(
            here.astype(jnp.int32).reshape(1),
            w_qkv.transpose(1, 0, 2),
            w_o,
            small.reshape(32, 128),
        ),
        "fsdp",
        axis=0,
        tiled=True,
    )
    small_all = first_pack[:, 1408:].reshape(8, shard, 128)[:, :32].reshape(8, 16, shard)
    small_all = small_all.transpose(1, 0, 2)
    bias_all = small_all[11, :, : 3 * bias_part].reshape(8, 3, bias_part)
    bias_all = wide(bias_all.transpose(1, 0, 2).reshape(1, 3 * head_size))
    small_all = small_all.reshape(16, width)
    gain_first, gain_second = wide(small_all[9]), wide(small_all[10])
    gate_rows = small_all[: experts + 1]
    small_rows = jnp.pad(gate_rows, ((0, 16 - experts - 1), (0, 0)))
    x_first = gather_first(inputs)
    x_second = gather_second(x_first)
    grad_own = low(wide(grad_out) * valid)
    grad_pack = jnp.concatenate(
        [grad_own, jnp.pad(low(chosen), ((0, 0), (0, 128 - experts)))], axis=1
    )
    here_late = after(here, (x_first, x_second, grad_pack, block_places))
    shared_start = after(here, x_first) * shared_units
    shared_gu = lax.dynamic_slice(w_sgu, (0, 0, shared_start), (shard, 2, shared_units))
    shared_gu = shared_gu.transpose(1, 2, 0)
    shared_down = lax.dynamic_slice(w_sdown, (0, shared_start), (shard, shared_units)).T
    expert_gu = lax.dynamic_index_in_dim(w_egu.transpose(1, 2, 3, 0), here_late, 0, keepdims=False)
    expert_down = lax.dynamic_index_in_dim(w_edown.transpose(1, 2, 0), here_late, 0, keepdims=False)
    unit_weights = lax.all_gather(
        jnp.concatenate(
            [expert_gu[0], shared_gu[0], expert_gu[1], shared_gu[1], expert_down, shared_down],
            axis=0,
        ),
        "fsdp",
        axis=0,
        tiled=False,
    )

    cosine, sine = rotary_tables(rows * 8, head_size)
    hidden_in = wide(inputs)
    x_blocks = gather_blocks(inputs, x_first, x_second)
    grad_pack = after(grad_pack, x_second)
    g_first = gather_first(grad_pack)
    g_second = gather_second(g_first)
    g_blocks = gather_blocks(grad_pack, g_first, g_second)
    queries, keys, values, attended, normed_first = attend(
        block_places, x_blocks, first_pack, gain_first[None], bias_all, cosine, sine
    )
    attended_own = lax.all_to_all(attended, "ctx", 0, 1, tiled=True)
    branch = add_halves(after(branch_part(attended_own, first_pack), g_first))
    middle = hidden_in + branch
    factor_second = inverse_rms(middle)
    normed_own = low(middle * factor_second * gain_second)

    n_first = gather_first(normed_own)
    n_second = gather_second(n_first)
    n_blocks = gather_blocks(normed_own, n_first, n_second)
    mine = (jnp.arange(16, dtype=jnp.int32) == here).astype(WIDE)[:, None]
    first_half, second_half = (0, 1, 2, 4), (3, 5, 6, 7)
    pick = lambda blocks, half: [blocks[index] for index in half]
    results = []
    for half in (first_half, second_half):
        results.append(
            units_forward_back(
                pick(n_blocks, half),
                pick(g_blocks, half),
                small_rows,
                mine,
                unit_weights,
                results[0][4:] if results else (),
            )
        )
    d_blocks = [None] * 8
    for half, result in zip((first_half, second_half), results):
        for place, index in enumerate(half):
            d_blocks[index] = result[place]
    back, hidden = results[1][4:]
    in_halves = lambda blocks: pick(blocks, first_half) + pick(blocks, second_half)
    weight_qkv_all = lax.all_gather(
        after(w_qkv.transpose(1, 0, 2), branch), "fsdp", axis=0, tiled=False
    )
    d_first = scatter_first(d_blocks)
    d_blocks[1:3] = after(d_blocks[1:3], (n_second, g_second))
    d_second = scatter_second(d_blocks, d_first)
    unit_part = outer_products(
        after(back, d_second[2:]),
        hidden,
        in_halves(n_blocks),
        in_halves(g_blocks),
    )
    unit_grads = lax.psum_scatter(unit_part, "fsdp", scatter_dimension=0, tiled=False)
    sums = scatter_sum(d_blocks[0], after(d_second, (unit_part, weight_qkv_all)))
    grad_sum = add_halves(sums[:, : width + 128])
    unit_first = large_first(unit_grads)

    logits = dot_rows(normed_own, gate_rows)
    probs_own = jax.nn.softmax(logits[:, :experts], axis=-1)
    gate_own = jax.nn.sigmoid(logits[:, experts : experts + 1])
    grad_normed, grad_combine = grad_sum[:, :width], grad_sum[:, width : width + experts]
    grad_gate = grad_sum[:, width + experts : width + experts + 1]
    picked = grad_combine * chosen
    grad_logits = low(
        probs_own * (picked - jnp.sum(picked * probs_own, axis=-1, keepdims=True))
    )
    grad_gate_logit = low(grad_gate * gate_own * (1.0 - gate_own))
    both = jnp.concatenate([grad_logits, grad_gate_logit], axis=1)
    grad_normed = grad_normed + dot_plain(both, gate_rows)
    grad_both = dot_columns(normed_own, both)
    grad_top = wide(grad_own)
    grad_gain_second = jnp.sum(grad_normed * middle * factor_second, axis=0)
    weighted = grad_normed * gain_second
    inner = jnp.mean(weighted * middle, axis=-1, keepdims=True)
    grad_middle = grad_top + weighted * factor_second - middle * factor_second**3 * inner
    grad_branch = low(grad_middle)

    grad_attended = branch_back(grad_branch, first_pack, heads * head_size)
    grad_heads = lax.all_to_all(
        grad_attended.reshape(rows, heads, head_size).transpose(1, 0, 2), "ctx", 0, 0, tiled=True
    ).reshape(rows * 8, head_size)
    grad_heads = after(grad_heads, unit_first)
    unit_second = large_second(unit_first)
    mixed = add_halves(after(sums[:, width + 128 :], grad_heads))
    result = low(valid * (middle + mixed))
    out_part = lax.psum_scatter(
        low(dot_columns(grad_branch, attended_own)), "fsdp", scatter_dimension=0, tiled=True
    )
    grad_proj, grad_bias = attend_back(queries, keys, values, grad_heads, cosine, sine)
    out_parts = out_part.reshape(shard, heads, head_size).transpose(1, 0, 2)
    out_parts = lax.all_to_all(after(out_parts, grad_proj), "ctx", 0, 0, tiled=True)
    grad_w_o_here = low(jnp.sum(wide(out_parts), axis=0))
    proj_own = lax.all_to_all(
        grad_proj.reshape(8, rows, 3 * head_size), "ctx", 0, 0, tiled=True
    )
    grad_qkv_here = low(dot_columns(normed_first, grad_proj))
    bias_rows = grad_bias.reshape(3, 8, bias_part).transpose(1, 0, 2).reshape(8, 3 * bias_part)
    bias_rows = jnp.pad(bias_rows, ((0, 0), (0, shard - 3 * bias_part))).reshape(width, 1)
    small_grads = low(jnp.concatenate([grad_both, grad_gain_second[:, None], bias_rows], axis=1))
    small_grads = jnp.pad(small_grads, ((0, 0), (0, 128 - small_grads.shape[1])))
    last_part = jnp.concatenate([grad_qkv_here, small_grads], axis=1)
    proj_own = after(proj_own, (last_part, unit_second, grad_w_o_here))
    proj_own = proj_own.reshape(8, rows, 3, head_size).transpose(2, 1, 0, 3)
    proj_own = proj_own.reshape(3, rows, heads * head_size)
    first_part = first_back(proj_own, weight_qkv_all)
    last_pack = lax.psum_scatter(last_part, "fsdp", scatter_dimension=0, tiled=True)
    weights_here = lax.dynamic_slice(
        w_qkv, (0, 0, here * head_size), (shard, 3, head_size)
    ).reshape(shard, 3 * head_size)
    products = jnp.sum(wide(weights_here) * wide(last_pack[:, : 3 * head_size]), axis=1)
    products = products + lax.ppermute(products, "tp", [(0, 1), (1, 0)])
    spare = 3 * head_size + experts + 3
    last_block = (
        jnp.concatenate(
            [
                last_pack[:, :spare],
                low(products)[:, None],
                last_pack[:, spare + 1 :],
                grad_w_o_here,
            ],
            axis=1,
        )
    )
    last_first = gather_first(last_block)
    unit_third = large_third(unit_second)
    grad_first = after(add_halves(after(first_part, last_first)), (result, unit_third))
    last_blocks = gather_blocks(last_block, last_first, gather_second(last_first))
    factor_first = inverse_rms(hidden_in)
    weighted = grad_first * gain_first
    inner = jnp.mean(weighted * hidden_in, axis=-1, keepdims=True)
    grad_input = grad_middle + weighted * factor_first - hidden_in * factor_first**3 * inner

    unit_blocks = large_blocks(unit_grads, unit_first, unit_second, unit_third)
    early, late = (0, 1, 2, 4), (3, 5, 6, 7)
    placed = ()
    for half in (early, late):
        block_half = after(block_places, unit_second)[jnp.array(half)]
        placed = place_units(block_half, pick(unit_blocks, half), expert_units, placed)
    grad_egu, grad_edown, shared_grads = placed
    grad_w_sgu, grad_w_sdown = flip(shared_grads.reshape(3, 8 * shared_units, shard))
    grad_qkv, grad_w_o, small_sums = place_last(block_places, last_blocks)
    grad_w_qkv = grad_qkv.transpose(1, 0, 2)
    summed = jnp.sum(small_sums[:, :, : experts + 4], axis=0)
    grad_b_qkv = (
        small_sums[:, : 3 * bias_part, experts + 2].reshape(8, 3, bias_part).transpose(1, 0, 2)
    )
    grad_gain_first = summed[:, experts + 3] / wide(norm_gains[0])
    return (
        result,
        low(grad_input),
        jnp.stack([grad_gain_first, summed[:, experts + 1]]),
        grad_w_qkv,
        grad_b_qkv,
        grad_w_o,
        summed[:, :experts],
        summed[:, experts],
        grad_w_sgu,
        grad_w_sdown,
        grad_egu.transpose(3, 0, 1, 2),
        grad_edown.transpose(2, 0, 1),
    )


def solution(mesh):
    return jax.shard_map(
        body,
        mesh=mesh,
        in_specs=(
            P(("fsdp", "ctx"), None),
            P(),
            P(("fsdp", "ctx"), None),
            P(None, "fsdp"),
            P("fsdp", None, "tp"),
            P(None, "tp", "fsdp"),
            P("fsdp", "tp"),
            P("fsdp", None),
            P("fsdp"),
            P("fsdp", None, "tp"),
            P("fsdp", "tp"),
            P("fsdp", None, None, "tp"),
            P("fsdp", None, "tp"),
            P(("fsdp", "ctx"), None),
        ),
        out_specs=(
            P(("fsdp", "ctx"), None),
            P(("fsdp", "ctx"), None),
            P(None, "fsdp"),
            P("fsdp", None, "tp"),
            P(None, "tp", "fsdp"),
            P("fsdp", "tp"),
            P("fsdp", None),
            P("fsdp"),
            P("fsdp", None, "tp"),
            P("fsdp", "tp"),
            P("fsdp", None, None, "tp"),
            P("fsdp", None, "tp"),
        ),
        check_vma=False,
    )
```
